512 devices in a mesh: seq: 16 (over x, y), fsdp: 32 (over z, core).
Axes of the slice: x: 4, y: 4, z: 16, core: 2. Of those that a mesh axis runs over, the one named last changes fastest.
Arguments:
- activations: bfloat16 [32, 4096, 2048], P('fsdp', 'seq'), may hold values from -6 to 6
- proj_weight: bfloat16 [2048, 2048], P('fsdp'), may hold values from -0.125 to 0.125
- gate_weight: bfloat16 [2048, 8], P('fsdp'), may hold values from -7.9549513 to 7.9549513
- forget_bias: float32 [4], replicated, may hold values from 5.2 to 11.5
- accepted: int32 [32], P('fsdp'), may hold values from 1024 to 4096, as said below
Outputs:
- hidden_out: bfloat16 [32, 4096, 1024], P('fsdp', 'seq')
The draws below stay inside these ranges and needn't reach their ends.
Inputs may be any that keep to these rules, and one draw needn't show every extreme that they name: Some sequence has accepted length 4096.
All inputs are finite; a program needn't handle non-finite values.
Results may differ from the reference program's by a relative error of at most 0.0074.
Values may be sent and summed in bfloat16 or wider, within the bound.
No kernel may reach another device: no remote copies, remote signals or barrier semaphores. Data moves between devices by JAX's collectives and lax.ppermute only.
A program may use at most 64 MiB of HBM per device.

```python
import jax
import jax.numpy as jnp
from jax import lax

D = 2048
H = 4
DK = 128
DV = 256
TOK_DEV = 256
LENGTH = 4096
SEQS = 32
N_SEQ = 16


def draw_gate_weight(key, part):
    key = jax.random.fold_in(key, 14)
    base_weight = jnp.clip(jax.random.normal(key, (D, 2 * H), jnp.float32), -6.0, 6.0) * (D // 4) ** (-0.5)
    return base_weight.astype(jnp.bfloat16)


def draw_forget_bias(key, part):
    key = jax.random.fold_in(key, 12)
    key_order, key_fast, key_slow = jax.random.split(key, 3)
    fast_heads = jax.random.permutation(key_order, H) < H // 2
    fast_bias = jax.random.uniform(key_fast, (H,), jnp.float32, 5.2, 6.2)
    slow_bias = jax.random.uniform(key_slow, (H,), jnp.float32, 10.0, 11.0)
    return jnp.where(fast_heads, fast_bias, slow_bias)


def draw_accepted(key, part):
    key = jax.random.fold_in(key, 13)
    key_length, key_order = jax.random.split(key)
    lengths = jax.random.randint(key_length, (SEQS,), LENGTH // 4, LENGTH + 1, dtype=jnp.int32)
    order = jax.random.permutation(key_order, SEQS)
    lengths = lengths.at[order[0]].set(LENGTH)
    lengths = lengths.at[order[1]].set(LENGTH // 4)
    return lengths.astype(jnp.int32)


def block_levels(key, extent, cuts, least, largest):
    level, own = 1.0, jax.random.fold_in(key, 6)
    for axis_at, parts in cuts:
        draws = jnp.exp(jax.random.uniform(jax.random.fold_in(own, axis_at), (parts,), jnp.float32, least / len(cuts), largest / len(cuts)))
        level = level * jnp.repeat(draws, extent[axis_at] // parts).reshape([-1 if axis == axis_at else 1 for axis in range(len(extent))])
    return level


def centred(rng, shape, spread, reach, cuts=(), held_as=jnp.bfloat16):
    entries = spread * jax.random.normal(rng, shape, jnp.float32)
    if cuts:
        entries = entries * block_levels(rng, shape, cuts, -0.22, 0.18)
    return jnp.clip(entries, -reach, reach).astype(held_as)


def setup_inputs(seed: int = 0) -> dict:
    key_list = jax.random.split(jax.random.key(seed), 6)
    return {
        "activations": centred(key_list[0], (SEQS, LENGTH, D), 1.0, 6.0, ((0, 32), (1, 16))),
        "proj_weight": centred(key_list[1], (D, H * (2 * DK + DV)), D ** -0.5, 0.125, ((0, 32),)),
        "gate_weight": draw_gate_weight(jax.random.fold_in(key_list[5], 71), 0),
        "forget_bias": draw_forget_bias(jax.random.fold_in(key_list[5], 71), 0),
        "accepted": draw_accepted(jax.random.fold_in(key_list[5], 71), 0),
    }


lowest = -1.0e30


def combine(earlier, later):
    total_a, top_a, memory_a, normal_a = earlier
    total_b, top_b, memory_b, normal_b = later
    top_log = jnp.maximum(total_b + top_a, top_b)
    scale_a = jnp.exp(total_b + top_a - top_log)
    scale_b = jnp.exp(top_b - top_log)
    return (total_a + total_b, top_log,
            scale_a[:, None, None] * memory_a + scale_b[:, None, None] * memory_b,
            scale_a[:, None] * normal_a + scale_b[:, None] * normal_b)


def gate_logs(gate_pre, forget_bias, live_rows):
    head_count = forget_bias.shape[0]
    input_pre = gate_pre[:, :head_count]
    forget_pre = gate_pre[:, head_count:] + forget_bias
    log_forget = jnp.where(live_rows[:, None], jax.nn.log_sigmoid(forget_pre), 0.0)
    log_input = jnp.where(live_rows[:, None], input_pre, lowest)
    return log_forget, log_input


def summarize(key_rows, value_entries, log_forget, log_input, live_rows):
    decay_sum = jnp.cumsum(log_forget, axis=0)
    total_log = decay_sum[-1]
    tail_log = total_log[None, :] - decay_sum + log_input
    top_log = jnp.max(tail_log, axis=0)
    scaling = jnp.where(live_rows[:, None], jnp.exp(tail_log - top_log[None, :]), 0.0)
    weighted_values = key_rows.astype(jnp.float32) * scaling[:, :, None]
    memory_matrix = jnp.einsum("lpz,lpu->pzu", weighted_values, value_entries.astype(jnp.float32),
                        precision=lax.Precision.HIGHEST)
    normal = jnp.sum(weighted_values, axis=0)
    return (total_log, top_log, memory_matrix, normal)


def block_output(query_rows, key_rows, value_entries, log_forget, log_input, live_rows, top_in, incoming_memory, normal_in):
    row_count = query_rows.shape[0]
    rescale_factor = query_rows.shape[2] ** -0.5
    decay_sum = jnp.cumsum(log_forget, axis=0).T
    log_weight = decay_sum[:, :, None] - decay_sum[:, None, :] + log_input.T[:, None, :]
    causal = jnp.arange(row_count)[:, None] >= jnp.arange(row_count)[None, :]
    log_weight = jnp.where(causal[None], log_weight, lowest)
    carried = decay_sum + top_in[:, None]
    top_row = jnp.maximum(jnp.max(log_weight, axis=2), carried)
    weights = jnp.exp(log_weight - top_row[:, :, None])
    carry_scale = jnp.exp(carried - top_row)
    query_broadened = query_rows.astype(jnp.float32)
    scores = jnp.einsum("thk,shk->hts", query_broadened, key_rows.astype(jnp.float32)) * rescale_factor
    products = weights * scores
    rounded = lax.optimization_barrier(products.astype(jnp.bfloat16)).astype(jnp.float32)
    denominator = jnp.sum(products, axis=2) + carry_scale * jnp.einsum(
        "thk,hk->ht", query_broadened, normal_in, precision=lax.Precision.HIGHEST) * rescale_factor
    numerator = jnp.einsum("hts,shv->thv", rounded, value_entries.astype(jnp.float32))
    numerator = numerator + carry_scale.T[:, :, None] * jnp.einsum(
        "ilq,lqg->ilg", query_broadened, incoming_memory, precision=lax.Precision.HIGHEST) * rescale_factor
    divisor = jnp.maximum(jnp.abs(denominator), 1.0).T
    result = jnp.where(live_rows[:, None, None], numerator / divisor[:, :, None], 0.0)
    return result.reshape(row_count, -1)


def reference(activations, proj_weight, gate_weight, forget_bias, accepted):
    def one_sequence(sequence_pair):
        sequence, length = sequence_pair
        blocks = sequence.reshape(N_SEQ, TOK_DEV, D)

        def advance(carry_state, scanned):
            block_rows, block_index = scanned
            projected = jnp.dot(block_rows, proj_weight, preferred_element_type=jnp.float32).astype(jnp.bfloat16)
            gate_pre = jnp.dot(block_rows, gate_weight, preferred_element_type=jnp.float32)
            positions = block_index * TOK_DEV + jnp.arange(TOK_DEV, dtype=jnp.int32)
            live_rows = positions < length
            log_forget, log_input = gate_logs(gate_pre, forget_bias, live_rows)
            query_rows = projected[:, :H * DK].reshape(TOK_DEV, H, DK)
            key_rows = projected[:, H * DK:2 * H * DK].reshape(TOK_DEV, H, DK)
            value_entries = projected[:, 2 * H * DK:].reshape(TOK_DEV, H, DV)
            output = block_output(query_rows, key_rows, value_entries, log_forget, log_input, live_rows,
                                  carry_state[1], carry_state[2], carry_state[3])
            summary = summarize(key_rows, value_entries, log_forget, log_input, live_rows)
            return combine(carry_state, summary), output.astype(jnp.bfloat16)

        initial = (jnp.zeros((H,), jnp.float32), jnp.full((H,), lowest, jnp.float32),
                   jnp.zeros((H, DK, DV), jnp.float32), jnp.zeros((H, DK), jnp.float32))
        final_state, outputs = lax.scan(advance, initial, (blocks, jnp.arange(N_SEQ, dtype=jnp.int32)))
        return outputs.reshape(LENGTH, H * DV)

    return lax.map(one_sequence, (activations, accepted))
```

```python
import functools

import jax
import jax.numpy as jnp
from jax import lax
from jax.experimental import pallas as pl
from jax.experimental.pallas import tpu as pltpu
from jax.sharding import Mesh
from jax.sharding import PartitionSpec as P

D = 2048
H = 4
DK = 128
DV = 256
TOK = 256
NX, NY, NZ, NC = 4, 4, 16, 2
QUAD = NY * TOK
HALF = D // (NZ * NC)
PIECE = HALF + 8
EXT = DV + 128
lowest = -1e30


def dot(a, b, contract=((1,), (0,))):
    return lax.dot_general(a, b, (contract, ((), ())), preferred_element_type=jnp.float32)


def split3(value):
    high = value.astype(jnp.bfloat16).astype(jnp.float32)
    rest = value - high
    middle = rest.astype(jnp.bfloat16).astype(jnp.float32)
    return high, middle, rest - middle


def scan_lanes(row, combine, neutral):
    size, step = row.shape[1], 1
    while step < size:
        pad = jnp.full((1, step), neutral, row.dtype)
        row = combine(row, jnp.concatenate([pad, row[:, : size - step]], axis=1))
        step *= 2
    return row


def project_kernel(
    info, bias, x_ref, own_ref, other_ref, q_ref, kt_ref, v_ref, rows_ref, sent_ref, weight, gate, pre
):
    block = pl.program_id(0)

    @pl.when(block == 0)
    def _():
        core = info[0]
        for part in range(4):
            for z in range(NZ):
                columns = pl.ds(part * 128, 128)
                weight[z, core, :, columns] = own_ref[part, z, :HALF, :]
                weight[z, 1 - core, :, columns] = other_ref[part, z, :HALF, :]
        mine = jnp.sum(own_ref[0, :, HALF:, :].astype(jnp.float32), axis=1)
        theirs = jnp.sum(other_ref[0, :, HALF:, :].astype(jnp.float32), axis=1)
        first = jnp.where(core == 0, mine, theirs)
        second = jnp.where(core == 0, theirs, mine)
        inputs = jnp.concatenate([first[:, :HALF], second[:, :HALF]], axis=1)
        forgets = jnp.concatenate([first[:, HALF:], second[:, HALF:]], axis=1)
        gate[...] = jnp.zeros_like(gate)
        for z in range(NZ):
            columns = pl.ds(z * 128, 128)
            gate[0:1, columns] = inputs[z : z + 1]
            gate[1:2, columns] = forgets[z : z + 1]

    tokens = x_ref[0]
    projected = dot(tokens, weight[...].reshape(D, 2 * DK + DV))
    here = pl.ds(pl.multiple_of(block * TOK, TOK), TOK)
    q_ref[here, :] = projected[:, :DK].astype(jnp.bfloat16)
    kt_ref[:, here] = projected[:, DK : 2 * DK].T.astype(jnp.bfloat16)
    v_ref[here, :] = projected[:, 2 * DK :].astype(jnp.bfloat16)
    pre[:, here] = dot(gate[...].astype(jnp.bfloat16), tokens, ((1,), (1,)))

    @pl.when(block == NY - 1)
    def _():
        accepted = info[1]
        positions = info[2] * QUAD + lax.broadcasted_iota(jnp.int32, (1, QUAD), 1)
        live = positions < accepted
        forget_pre = pre[1:2, :] + bias[0]
        log_sigmoid = jnp.minimum(forget_pre, 0.0) - jnp.log1p(jnp.exp(-jnp.abs(forget_pre)))
        log_forget = jnp.where(live, log_sigmoid, 0.0)
        log_input = jnp.where(live, pre[0:1, :], lowest)
        decay_sum = scan_lanes(log_forget, jnp.add, 0.0)
        relative = log_input - decay_sum
        running_top = scan_lanes(relative, jnp.maximum, lowest)
        total = decay_sum[:, QUAD - 1 :]
        last_top = running_top[:, QUAD - 1 :]
        rows_ref[...] = jnp.concatenate(
            [relative, running_top, jnp.zeros((6, QUAD), jnp.float32)], axis=0
        )
        scaling = jnp.where(live, jnp.exp(relative - last_top), 0.0)
        weighted = (kt_ref[...].astype(jnp.float32) * scaling).astype(jnp.bfloat16)
        lane = lax.broadcasted_iota(jnp.int32, (QUAD, 128), 1)
        ones = jnp.where(lane == 0, 1.0, 0.0).astype(jnp.bfloat16)
        memory = dot(weighted, v_ref[...])
        normal = dot(weighted, ones)
        lane = lax.broadcasted_iota(jnp.int32, (DK, 128), 1)
        logs = normal
        for at, value in enumerate((*split3(total), *split3(total + last_top))):
            logs = jnp.where(lane == at + 1, value, logs)
        for to in range(NX):
            sent_ref[to, :, :DV] = memory.astype(jnp.bfloat16)
            sent_ref[to, :, DV:] = logs.astype(jnp.bfloat16)


def cell_kernel(info, q_ref, kt_ref, v_ref, rows_ref, states_ref, out_ref, carried, top_in):
    block = pl.program_id(0)

    @pl.when(block == 0)
    def _():
        place = info[2]
        state = jnp.zeros((DK, EXT), jnp.float32)
        top = jnp.full((1, 1), lowest, jnp.float32)
        for source in range(NX - 1):
            entry = states_ref[source].astype(jnp.float32)
            logs = entry[0:1, DV:]
            total = logs[:, 1:2] + (logs[:, 2:3] + logs[:, 3:4])
            top_part = logs[:, 4:5] + (logs[:, 5:6] + logs[:, 6:7])
            top_new = jnp.maximum(total + top, top_part)
            joined = jnp.exp(total + top - top_new) * state + jnp.exp(top_part - top_new) * entry
            state = jnp.where(source < place, joined, state)
            top = jnp.where(source < place, top_new, top)
        carried[...] = state.astype(jnp.bfloat16)
        top_in[...] = jnp.broadcast_to(top, (8, 128))

    scale = DK**-0.5
    carry_top = top_in[0:1, 0:1]
    for own in range(NY):

        @pl.when(block == own)
        def _():
            here = pl.ds(own * TOK, TOK)
            extent = (own + 1) * TOK
            columns = rows_ref[:, here].T
            top = jnp.maximum(columns[:, 1:2], carry_top)
            queries = q_ref[here, :]
            scores = dot(queries, kt_ref[:, :extent]) * scale
            relative = rows_ref[0:1, :extent] - top
            row = own * TOK + lax.broadcasted_iota(jnp.int32, (TOK, extent), 0)
            column = lax.broadcasted_iota(jnp.int32, (TOK, extent), 1)
            products = jnp.exp(jnp.where(row >= column, relative, lowest)) * scores
            carry = dot(queries, carried[...]) * (jnp.exp(carry_top - top) * scale)
            denominator = jnp.sum(products, axis=1, keepdims=True) + carry[:, DV : DV + 1]
            numerator = dot(products.astype(jnp.bfloat16), v_ref[:extent, :]) + carry[:, :DV]
            result = numerator / jnp.maximum(jnp.abs(denominator), 1.0)
            position = info[2] * QUAD + own * TOK + lax.broadcasted_iota(jnp.int32, (TOK, 1), 0)
            out_ref[0] = jnp.where(position < info[1], result, 0.0).astype(jnp.bfloat16)


SMEM = pl.BlockSpec(memory_space=pltpu.SMEM)


def whole(*shape):
    return pl.BlockSpec(shape, lambda block: (0,) * len(shape))


def project(info, bias, quad, own, other, **options):
    return pl.pallas_call(
        project_kernel,
        grid=(NY,),
        out_shape=(
            jax.ShapeDtypeStruct((QUAD, DK), jnp.bfloat16),
            jax.ShapeDtypeStruct((DK, QUAD), jnp.bfloat16),
            jax.ShapeDtypeStruct((QUAD, DV), jnp.bfloat16),
            jax.ShapeDtypeStruct((8, QUAD), jnp.float32),
            jax.ShapeDtypeStruct((NX, DK, EXT), jnp.bfloat16),
        ),
        in_specs=[
            SMEM,
            SMEM,
            pl.BlockSpec((1, TOK, D), lambda block: (block, 0, 0)),
            whole(4, NZ, PIECE, 128),
            whole(4, NZ, PIECE, 128),
        ],
        out_specs=(
            whole(QUAD, DK),
            whole(DK, QUAD),
            whole(QUAD, DV),
            whole(8, QUAD),
            whole(NX, DK, EXT),
        ),
        scratch_shapes=[
            pltpu.VMEM((NZ, NC, HALF, 2 * DK + DV), jnp.bfloat16),
            pltpu.VMEM((8, D), jnp.float32),
            pltpu.VMEM((8, QUAD), jnp.float32),
        ],
        compiler_params=pltpu.CompilerParams(vmem_limit_bytes=40 * 1024 * 1024),
        name="project",
        **options,
    )(info, bias, quad, own, other)


def cell(info, q, kt, v, rows, states, **options):
    return pl.pallas_call(
        cell_kernel,
        grid=(NY,),
        out_shape=jax.ShapeDtypeStruct((NY, TOK, DV), jnp.bfloat16),
        in_specs=[
            SMEM,
            whole(QUAD, DK),
            whole(DK, QUAD),
            whole(QUAD, DV),
            whole(8, QUAD),
            whole(NX, DK, EXT),
        ],
        out_specs=pl.BlockSpec((1, TOK, DV), lambda block: (block, 0, 0)),
        scratch_shapes=[pltpu.VMEM((DK, EXT), jnp.bfloat16), pltpu.VMEM((8, 128), jnp.float32)],
        compiler_params=pltpu.CompilerParams(vmem_limit_bytes=40 * 1024 * 1024),
        name="cell",
        **options,
    )(info, q, kt, v, rows, states)


def weight_piece(proj_weight, gate_weight, x, y):
    quarter = jnp.stack([y, H + y, 2 * H + 2 * y, 2 * H + 2 * y + 1])[x]
    columns = lax.dynamic_slice(proj_weight, (0, quarter * 128), (HALF, 128))
    pair = [lax.dynamic_slice(gate_weight, (0, at), (HALF, 1)) for at in (y, H + y)]
    row = jnp.concatenate(pair, axis=0).reshape(1, 2 * HALF)
    return jnp.concatenate([columns, row, jnp.zeros((7, 128), row.dtype)], axis=0)


def per_device(activations, proj_weight, gate_weight, forget_bias, accepted):
    x, y, core = (lax.axis_index(a) for a in ("x", "y", "c"))
    quad = lax.all_gather(activations, "y", axis=0, tiled=True)
    piece = weight_piece(proj_weight, gate_weight, x, y)
    rows = lax.all_to_all(jnp.tile(piece, (NZ, 1)), "z", 0, 0, tiled=True)
    own = lax.all_to_all(jnp.tile(rows, (NX, 1)), "x", 0, 0, tiled=True)
    other = lax.ppermute(own, "c", [(0, 1), (1, 0)])
    shape = (4, NZ, PIECE, 128)
    info = jnp.stack([core, accepted[0], x]).astype(jnp.int32)
    bias = lax.dynamic_slice(forget_bias, (y,), (1,))
    q, kt, v, gates, sent = project(info, bias, quad, own.reshape(shape), other.reshape(shape))
    states = lax.all_to_all(sent, "x", 0, 0, tiled=True)
    out = cell(info, q, kt, v, gates, states)
    heads = lax.all_to_all(out, "y", 0, 0, tiled=True)
    return heads.transpose(1, 0, 2).reshape(1, TOK, H * DV)


def solution(mesh):
    axes = Mesh(mesh.devices.reshape(NX, NY, NZ, NC), ("x", "y", "z", "c"))
    tokens = P(("z", "c"), ("x", "y"), None)
    weights = P(("z", "c"), None)
    return jax.shard_map(
        per_device,
        mesh=axes,
        in_specs=(tokens, weights, weights, P(), P(("z", "c"))),
        out_specs=tokens,
        check_vma=False,
    )
```

```python
import functools

import jax
import jax.numpy as jnp
from jax import lax
from jax.experimental import pallas as pl
from jax.experimental.pallas import tpu as pltpu
from jax.sharding import Mesh
from jax.sharding import PartitionSpec as P

D = 2048
H = 4
DK = 128
DV = 256
TOK = 256
NX, NY, NZ, NC = 4, 4, 16, 2
QUAD = NY * TOK
HALF = D // (NZ * NC)
PIECE = HALF + 8
EXT = DV + 128
lowest = -1e30


def dot(a, b, contract=((1,), (0,))):
    return lax.dot_general(a, b, (contract, ((), ())), preferred_element_type=jnp.float32)


def split3(value):
    high = value.astype(jnp.bfloat16).astype(jnp.float32)
    rest = value - high
    middle = rest.astype(jnp.bfloat16).astype(jnp.float32)
    return high, middle, rest - middle


def scan_row(row, combine, neutral):
    lane = lax.broadcasted_iota(jnp.int32, (8, 128), 1)
    sub = lax.broadcasted_iota(jnp.int32, (8, 128), 0)
    chunk = jnp.concatenate([row[:, at * 128 : at * 128 + 128] for at in range(QUAD // 128)], axis=0)
    for step in (1, 2, 4, 8, 16, 32, 64):
        chunk = combine(chunk, jnp.where(lane >= step, pltpu.roll(chunk, step, 1), neutral))
    before = jnp.broadcast_to(chunk[:, 127:], (8, 128))
    before = jnp.where(sub >= 1, pltpu.roll(before, 1, 0), neutral)
    for step in (1, 2, 4):
        before = combine(before, jnp.where(sub >= step, pltpu.roll(before, step, 0), neutral))
    chunk = combine(chunk, before)
    return jnp.concatenate([chunk[at : at + 1, :] for at in range(QUAD // 128)], axis=1)


def assemble_kernel(info, own_ref, other_ref, weight_ref, gate_ref):
    core = info[0]
    for part in range(4):
        for z in range(NZ):
            columns = pl.ds(part * 128, 128)
            weight_ref[z, core, :, columns] = own_ref[part, z, :HALF, :]
            weight_ref[z, 1 - core, :, columns] = other_ref[part, z, :HALF, :]
    mine = jnp.sum(own_ref[0, :, HALF:, :].astype(jnp.float32), axis=1)
    theirs = jnp.sum(other_ref[0, :, HALF:, :].astype(jnp.float32), axis=1)
    first = jnp.where(core == 0, mine, theirs)
    second = jnp.where(core == 0, theirs, mine)
    inputs = jnp.concatenate([first[:, :HALF], second[:, :HALF]], axis=1)
    forgets = jnp.concatenate([first[:, HALF:], second[:, HALF:]], axis=1)
    gate_ref[...] = jnp.zeros_like(gate_ref)
    for z in range(NZ):
        columns = pl.ds(z * 128, 128)
        gate_ref[0:1, columns] = inputs[z : z + 1]
        gate_ref[1:2, columns] = forgets[z : z + 1]


def project_kernel(
    info, bias, x_hbm, weight_ref, gate_ref, q_ref, kt_ref, v_ref, rows_ref, sent_ref, tokens, arrived
):
    copies = [
        pltpu.make_async_copy(x_hbm.at[block], tokens.at[block], arrived.at[block])
        for block in range(NY)
    ]
    for copy in copies:
        copy.start()
    weight = weight_ref[...].reshape(D, 2 * DK + DV)
    gate = gate_ref[...].astype(jnp.bfloat16)
    pre = []
    for block in range(NY):
        copies[block].wait()
        here = pl.ds(block * TOK, TOK)
        pre.append(dot(gate, tokens[block], ((1,), (1,))))
        projected = dot(tokens[block], weight)
        q_ref[here, :] = projected[:, :DK].astype(jnp.bfloat16)
        kt_ref[:, here] = projected[:, DK : 2 * DK].T.astype(jnp.bfloat16)
        v_ref[here, :] = projected[:, 2 * DK :].astype(jnp.bfloat16)
    pre = jnp.concatenate(pre, axis=1)

    accepted = info[1]
    positions = info[2] * QUAD + lax.broadcasted_iota(jnp.int32, (1, QUAD), 1)
    live = positions < accepted
    forget_pre = pre[1:2, :] + bias[0]
    log_sigmoid = jnp.minimum(forget_pre, 0.0) - jnp.log1p(jnp.exp(-jnp.abs(forget_pre)))
    log_forget = jnp.where(live, log_sigmoid, 0.0)
    log_input = jnp.where(live, pre[0:1, :], lowest)
    decay_sum = scan_row(log_forget, jnp.add, 0.0)
    relative = log_input - decay_sum
    running_top = scan_row(relative, jnp.maximum, 2 * lowest)
    total = decay_sum[:, QUAD - 1 :]
    last_top = running_top[:, QUAD - 1 :]
    rows_ref[...] = jnp.concatenate(
        [relative, running_top, jnp.zeros((6, QUAD), jnp.float32)], axis=0
    )
    scaling = jnp.where(live, jnp.exp(relative - last_top), 0.0)
    weighted = kt_ref[...].astype(jnp.float32) * scaling
    normal = jnp.sum(weighted, axis=1, keepdims=True)
    memory = dot(weighted.astype(jnp.bfloat16), v_ref[...])
    lane = lax.broadcasted_iota(jnp.int32, (DK, 128), 1)
    logs = jnp.where(lane == 0, normal, 0.0)
    for at, value in enumerate((*split3(total), *split3(total + last_top))):
        logs = jnp.where(lane == at + 1, value, logs)
    sent_ref[:, :DV] = memory.astype(jnp.bfloat16)
    sent_ref[:, DV:] = logs.astype(jnp.bfloat16)


def cell_kernel(swaps, info, q_ref, kt_ref, v_ref, rows_ref, *refs):
    state_refs, out_refs = refs[: NX - 1], refs[NX - 1 :]
    place = info[2]
    state = jnp.zeros((DK, EXT), jnp.float32)
    carry_top = jnp.full((1, 1), lowest, jnp.float32)
    for distance in range(NX - 1, 0, -1):
        entry = state_refs[distance - 1][...].astype(jnp.float32)
        logs = entry[0:1, DV:]
        total = logs[:, 1:2] + (logs[:, 2:3] + logs[:, 3:4])
        top_part = logs[:, 4:5] + (logs[:, 5:6] + logs[:, 6:7])
        top_new = jnp.maximum(total + carry_top, top_part)
        joined = jnp.exp(total + carry_top - top_new) * state + jnp.exp(top_part - top_new) * entry
        state = jnp.where(place >= distance, joined, state)
        carry_top = jnp.where(place >= distance, top_new, carry_top)
    carried = state.astype(jnp.bfloat16)

    scale = DK**-0.5
    for swap, out_ref in zip(swaps, out_refs, strict=True):
        block = jnp.bitwise_xor(info[3], swap)
        for own in range(NY):

            @pl.when(block == own)
            def _(own=own, out_ref=out_ref):
                here = pl.ds(own * TOK, TOK)
                extent = (own + 1) * TOK
                columns = rows_ref[:, here].T
                top = jnp.maximum(columns[:, 1:2], carry_top)
                queries = q_ref[here, :]
                scores = dot(queries, kt_ref[:, :extent]) * scale
                relative = rows_ref[0:1, :extent] - top
                row = own * TOK + lax.broadcasted_iota(jnp.int32, (TOK, extent), 0)
                column = lax.broadcasted_iota(jnp.int32, (TOK, extent), 1)
                products = jnp.exp(jnp.where(row >= column, relative, lowest)) * scores
                carry = dot(queries, carried) * (jnp.exp(carry_top - top) * scale)
                denominator = jnp.sum(products, axis=1, keepdims=True) + carry[:, DV : DV + 1]
                numerator = dot(products.astype(jnp.bfloat16), v_ref[:extent, :]) + carry[:, :DV]
                result = numerator / jnp.maximum(jnp.abs(denominator), 1.0)
                at = place * QUAD + own * TOK + lax.broadcasted_iota(jnp.int32, (TOK, 1), 0)
                out_ref[...] = jnp.where(at < info[1], result, 0.0).astype(jnp.bfloat16)


def merge_kernel(info, *refs):
    for swap in range(H):
        head = jnp.bitwise_xor(info[3], swap)
        columns = pl.ds(pl.multiple_of(head * DV, DV), DV)
        refs[H][0, :, columns] = refs[swap][...]


SMEM = pl.BlockSpec(memory_space=pltpu.SMEM)
VMEM = pl.BlockSpec(memory_space=pltpu.VMEM)
PARAMS = pltpu.CompilerParams(vmem_limit_bytes=56 * 1024 * 1024)


def shaped(*shape, dtype=jnp.bfloat16):
    return jax.ShapeDtypeStruct(shape, dtype)


def assemble(info, own, other, **options):
    return pl.pallas_call(
        assemble_kernel,
        out_shape=(shaped(NZ, NC, HALF, 2 * DK + DV), shaped(8, D, dtype=jnp.float32)),
        in_specs=[SMEM, VMEM, VMEM],
        out_specs=(VMEM, VMEM),
        compiler_params=PARAMS,
        name="assemble",
        **options,
    )(info, own, other)


def project(info, bias, quad, weight, gate, **options):
    return pl.pallas_call(
        project_kernel,
        out_shape=(
            shaped(QUAD, DK),
            shaped(DK, QUAD),
            shaped(QUAD, DV),
            shaped(8, QUAD, dtype=jnp.float32),
            shaped(DK, EXT),
        ),
        in_specs=[SMEM, SMEM, pl.BlockSpec(memory_space=pl.ANY), VMEM, VMEM],
        out_specs=(VMEM,) * 5,
        scratch_shapes=[
            pltpu.VMEM((NY, TOK, D), jnp.bfloat16),
            pltpu.SemaphoreType.DMA((NY,)),
        ],
        compiler_params=PARAMS,
        name="project",
        **options,
    )(info, bias, quad, weight, gate)


def cell(swaps, info, q, kt, v, rows, states, **options):
    return pl.pallas_call(
        functools.partial(cell_kernel, swaps),
        out_shape=(shaped(TOK, DV),) * len(swaps),
        in_specs=[SMEM] + [VMEM] * (4 + len(states)),
        out_specs=(VMEM,) * len(swaps),
        compiler_params=PARAMS,
        name="cell",
        **options,
    )(info, q, kt, v, rows, *states)


def merge(info, heads, **options):
    return pl.pallas_call(
        merge_kernel,
        out_shape=shaped(1, TOK, H * DV),
        in_specs=[SMEM] + [VMEM] * H,
        out_specs=VMEM,
        compiler_params=PARAMS,
        name="merge",
        **options,
    )(info, *heads)


def weight_piece(proj_weight, gate_weight, x, y):
    quarter = jnp.stack([y, H + y, 2 * H + 2 * y, 2 * H + 2 * y + 1])[x]
    columns = lax.dynamic_slice(proj_weight, (0, quarter * 128), (HALF, 128))
    pair = [lax.dynamic_slice(gate_weight, (0, at), (HALF, 1)) for at in (y, H + y)]
    row = jnp.concatenate(pair, axis=0).reshape(1, 2 * HALF)
    return jnp.concatenate([columns, row, jnp.zeros((7, 128), row.dtype)], axis=0)


def per_device(activations, proj_weight, gate_weight, forget_bias, accepted):
    x, y, core = (lax.axis_index(a) for a in ("x", "y", "c"))
    quad = lax.all_gather(activations, "y", axis=0, tiled=True)
    piece = weight_piece(proj_weight, gate_weight, x, y)
    rows = lax.all_to_all(jnp.tile(piece, (NZ, 1)), "z", 0, 0, tiled=True)
    own = lax.all_to_all(jnp.tile(rows, (NX, 1)), "x", 0, 0, tiled=True)
    other = lax.ppermute(own, "c", [(0, 1), (1, 0)])
    shape = (4, NZ, PIECE, 128)
    info = jnp.stack([core, accepted[0], x, y]).astype(jnp.int32)
    bias = lax.dynamic_slice(forget_bias, (y,), (1,))
    weight, gate = assemble(info, own.reshape(shape), other.reshape(shape))
    q, kt, v, gates, sent = project(info, bias, quad, weight, gate)
    states = [
        lax.ppermute(sent, "x", [(i, i + distance) for i in range(NX - distance)])
        for distance in range(1, NX)
    ]
    parts = (info, q, kt, v, gates, states)
    theirs = cell((2, 1, 3), *parts)
    swapped = {
        swap: lax.ppermute(part, "y", [(i, i ^ swap) for i in range(NY)])
        for swap, part in zip((2, 1, 3), theirs, strict=True)
    }
    (mine,) = cell((0,), *parts)
    return merge(info, [mine, swapped[1], swapped[2], swapped[3]])


def solution(mesh):
    axes = Mesh(mesh.devices.reshape(NX, NY, NZ, NC), ("x", "y", "z", "c"))
    tokens = P(("z", "c"), ("x", "y"), None)
    weights = P(("z", "c"), None)
    return jax.shard_map(
        per_device,
        mesh=axes,
        in_specs=(tokens, weights, weights, P(), P(("z", "c"))),
        out_specs=tokens,
        check_vma=False,
    )
```

```python
import jax
import jax.numpy as jnp
from jax import lax
from jax.experimental import pallas as pl
from jax.experimental.pallas import tpu as pltpu
from jax.sharding import Mesh
from jax.sharding import PartitionSpec as P

D = 2048
H = 4
DK = 128
DV = 256
TOK = 256
NX, NY, NZ, NC = 4, 4, 16, 2
QUAD = NY * TOK
HALF = D // (NZ * NC)
PIECE = HALF + 8
EXT = DV + 128
lowest = -1e30


def dot(a, b, contract=((1,), (0,))):
    return lax.dot_general(a, b, (contract, ((), ())), preferred_element_type=jnp.float32)


def split3(value):
    high = value.astype(jnp.bfloat16).astype(jnp.float32)
    rest = value - high
    middle = rest.astype(jnp.bfloat16).astype(jnp.float32)
    return high, middle, rest - middle


def scan_row(row, combine, neutral):
    lane = lax.broadcasted_iota(jnp.int32, (8, 128), 1)
    sub = lax.broadcasted_iota(jnp.int32, (8, 128), 0)
    chunk = jnp.concatenate([row[:, at * 128 : at * 128 + 128] for at in range(QUAD // 128)], axis=0)
    for step in (1, 2, 4, 8, 16, 32, 64):
        chunk = combine(chunk, jnp.where(lane >= step, pltpu.roll(chunk, step, 1), neutral))
    before = jnp.broadcast_to(chunk[:, 127:], (8, 128))
    before = jnp.where(sub >= 1, pltpu.roll(before, 1, 0), neutral)
    for step in (1, 2, 4):
        before = combine(before, jnp.where(sub >= step, pltpu.roll(before, step, 0), neutral))
    chunk = combine(chunk, before)
    return jnp.concatenate([chunk[at : at + 1, :] for at in range(QUAD // 128)], axis=1)


def assemble_kernel(info, own_ref, other_ref, weight_ref, gate_ref):
    core = info[0]
    for part in range(4):
        for z in range(NZ):
            columns = pl.ds(part * 128, 128)
            weight_ref[z, core, :, columns] = own_ref[part, z, :HALF, :]
            weight_ref[z, 1 - core, :, columns] = other_ref[part, z, :HALF, :]
    mine = jnp.sum(own_ref[0, :, HALF:, :].astype(jnp.float32), axis=1)
    theirs = jnp.sum(other_ref[0, :, HALF:, :].astype(jnp.float32), axis=1)
    first = jnp.where(core == 0, mine, theirs)
    second = jnp.where(core == 0, theirs, mine)
    inputs = jnp.concatenate([first[:, :HALF], second[:, :HALF]], axis=1)
    forgets = jnp.concatenate([first[:, HALF:], second[:, HALF:]], axis=1)
    gate_ref[...] = jnp.zeros_like(gate_ref)
    for z in range(NZ):
        columns = pl.ds(z * 128, 128)
        gate_ref[0:1, columns] = inputs[z : z + 1]
        gate_ref[1:2, columns] = forgets[z : z + 1]


def project_kernel(
    info, bias, x_hbm, weight_ref, gate_ref, q_ref, kt_ref, v_ref, rows_ref, sent_ref, tokens, arrived
):
    copies = [
        pltpu.make_async_copy(x_hbm.at[block], tokens.at[block], arrived.at[block])
        for block in range(NY)
    ]
    for copy in copies:
        copy.start()
    weight = weight_ref[...].reshape(D, 2 * DK + DV)
    gate = gate_ref[...].astype(jnp.bfloat16)
    pre = []
    for block in range(NY):
        copies[block].wait()
        here = pl.ds(block * TOK, TOK)
        pre.append(dot(gate, tokens[block], ((1,), (1,))))
        projected = dot(tokens[block], weight)
        q_ref[here, :] = projected[:, :DK].astype(jnp.bfloat16)
        kt_ref[:, here] = projected[:, DK : 2 * DK].T.astype(jnp.bfloat16)
        v_ref[here, :] = projected[:, 2 * DK :].astype(jnp.bfloat16)
    pre = jnp.concatenate(pre, axis=1)

    accepted = info[1]
    positions = info[2] * QUAD + lax.broadcasted_iota(jnp.int32, (1, QUAD), 1)
    live = positions < accepted
    forget_pre = pre[1:2, :] + bias[0]
    log_sigmoid = jnp.minimum(forget_pre, 0.0) - jnp.log1p(jnp.exp(-jnp.abs(forget_pre)))
    log_forget = jnp.where(live, log_sigmoid, 0.0)
    log_input = jnp.where(live, pre[0:1, :], lowest)
    decay_sum = scan_row(log_forget, jnp.add, 0.0)
    relative = log_input - decay_sum
    running_top = scan_row(relative, jnp.maximum, 2 * lowest)
    total = decay_sum[:, QUAD - 1 :]
    last_top = running_top[:, QUAD - 1 :]
    rows_ref[...] = jnp.concatenate(
        [relative, running_top, jnp.zeros((6, QUAD), jnp.float32)], axis=0
    )
    scaling = jnp.where(live, jnp.exp(relative - last_top), 0.0)
    weighted = kt_ref[...].astype(jnp.float32) * scaling
    normal = jnp.sum(weighted, axis=1, keepdims=True)
    memory = dot(weighted.astype(jnp.bfloat16), v_ref[...])
    lane = lax.broadcasted_iota(jnp.int32, (DK, 128), 1)
    logs = jnp.where(lane == 0, normal, 0.0)
    for at, value in enumerate((*split3(total), *split3(total + last_top))):
        logs = jnp.where(lane == at + 1, value, logs)
    for to in range(NX):
        sent_ref[to, :, :DV] = memory.astype(jnp.bfloat16)
        sent_ref[to, :, DV:] = logs.astype(jnp.bfloat16)


def cell_kernel(info, q_ref, kt_ref, v_ref, rows_ref, states_ref, out_ref):
    place = info[2]
    state = jnp.zeros((DK, EXT), jnp.float32)
    carry_top = jnp.full((1, 1), lowest, jnp.float32)
    for source in range(NX - 1):
        entry = states_ref[source].astype(jnp.float32)
        logs = entry[0:1, DV:]
        total = logs[:, 1:2] + (logs[:, 2:3] + logs[:, 3:4])
        top_part = logs[:, 4:5] + (logs[:, 5:6] + logs[:, 6:7])
        top_new = jnp.maximum(total + carry_top, top_part)
        joined = jnp.exp(total + carry_top - top_new) * state + jnp.exp(top_part - top_new) * entry
        state = jnp.where(source < place, joined, state)
        carry_top = jnp.where(source < place, top_new, carry_top)
    carried = state.astype(jnp.bfloat16)

    scale = DK**-0.5
    columns = rows_ref[...].T
    for block in range(NY):
        here = pl.ds(block * TOK, TOK)
        extent = (block + 1) * TOK
        top = jnp.maximum(columns[block * TOK : extent, 1:2], carry_top)
        queries = q_ref[here, :]
        scores = dot(queries, kt_ref[:, :extent]) * scale
        relative = rows_ref[0:1, :extent] - top
        row = block * TOK + lax.broadcasted_iota(jnp.int32, (TOK, extent), 0)
        column = lax.broadcasted_iota(jnp.int32, (TOK, extent), 1)
        products = jnp.exp(jnp.where(row >= column, relative, lowest)) * scores
        carry = dot(queries, carried) * (jnp.exp(carry_top - top) * scale)
        denominator = jnp.sum(products, axis=1, keepdims=True) + carry[:, DV : DV + 1]
        numerator = dot(products.astype(jnp.bfloat16), v_ref[:extent, :]) + carry[:, :DV]
        result = numerator / jnp.maximum(jnp.abs(denominator), 1.0)
        at = place * QUAD + block * TOK + lax.broadcasted_iota(jnp.int32, (TOK, 1), 0)
        out_ref[block] = jnp.where(at < info[1], result, 0.0).astype(jnp.bfloat16)


def merge_kernel(heads_ref, out_ref):
    for head in range(H):
        out_ref[0, :, head * DV : (head + 1) * DV] = heads_ref[head]


SMEM = pl.BlockSpec(memory_space=pltpu.SMEM)
VMEM = pl.BlockSpec(memory_space=pltpu.VMEM)


def granted(mebibytes):
    return pltpu.CompilerParams(vmem_limit_bytes=mebibytes * 1024 * 1024)


def shaped(*shape, dtype=jnp.bfloat16):
    return jax.ShapeDtypeStruct(shape, dtype)


def assemble(info, own, other, **options):
    return pl.pallas_call(
        assemble_kernel,
        out_shape=(shaped(NZ, NC, HALF, 2 * DK + DV), shaped(8, D, dtype=jnp.float32)),
        in_specs=[SMEM, VMEM, VMEM],
        out_specs=(VMEM, VMEM),
        compiler_params=granted(16),
        name="assemble",
        **options,
    )(info, own, other)


def project(info, bias, quad, weight, gate, **options):
    return pl.pallas_call(
        project_kernel,
        out_shape=(
            shaped(QUAD, DK),
            shaped(DK, QUAD),
            shaped(QUAD, DV),
            shaped(8, QUAD, dtype=jnp.float32),
            shaped(NX, DK, EXT),
        ),
        in_specs=[SMEM, SMEM, pl.BlockSpec(memory_space=pltpu.HBM), VMEM, VMEM],
        out_specs=(VMEM,) * 5,
        scratch_shapes=[
            pltpu.VMEM((NY, TOK, D), jnp.bfloat16),
            pltpu.SemaphoreType.DMA((NY,)),
        ],
        compiler_params=granted(24),
        name="project",
        **options,
    )(info, bias, quad, weight, gate)


def cell(info, q, kt, v, rows, states, **options):
    return pl.pallas_call(
        cell_kernel,
        out_shape=shaped(NY, TOK, DV),
        in_specs=[SMEM] + [VMEM] * 5,
        out_specs=VMEM,
        compiler_params=granted(16),
        name="cell",
        **options,
    )(info, q, kt, v, rows, states)


def merge(heads, **options):
    return pl.pallas_call(
        merge_kernel,
        out_shape=shaped(1, TOK, H * DV),
        in_specs=[VMEM],
        out_specs=VMEM,
        compiler_params=granted(8),
        name="merge",
        **options,
    )(heads)


def weight_piece(proj_weight, gate_weight, x, y):
    quarter = jnp.stack([y, H + y, 2 * H + 2 * y, 2 * H + 2 * y + 1])[x]
    columns = lax.dynamic_slice(proj_weight, (0, quarter * 128), (HALF, 128))
    pair = [lax.dynamic_slice(gate_weight, (0, at), (HALF, 1)) for at in (y, H + y)]
    row = jnp.concatenate(pair, axis=0).reshape(1, 2 * HALF)
    return jnp.concatenate([columns, row, jnp.zeros((7, 128), row.dtype)], axis=0)


def per_device(activations, proj_weight, gate_weight, forget_bias, accepted):
    x, y, core = (lax.axis_index(a) for a in ("x", "y", "c"))
    quad = lax.all_gather(activations, "y", axis=0, tiled=True)
    piece = weight_piece(proj_weight, gate_weight, x, y)
    rows = lax.all_to_all(jnp.tile(piece, (NZ, 1)), "z", 0, 0, tiled=True)
    own = lax.all_to_all(jnp.tile(rows, (NX, 1)), "x", 0, 0, tiled=True)
    other = lax.ppermute(own, "c", [(0, 1), (1, 0)])
    shape = (4, NZ, PIECE, 128)
    info = jnp.stack([core, accepted[0], x]).astype(jnp.int32)
    bias = lax.dynamic_slice(forget_bias, (y,), (1,))
    weight, gate = assemble(info, own.reshape(shape), other.reshape(shape))
    q, kt, v, gates, sent = project(info, bias, quad, weight, gate)
    states = lax.all_to_all(sent, "x", 0, 0, tiled=True)
    out = cell(info, q, kt, v, gates, states)
    return merge(lax.all_to_all(out, "y", 0, 0, tiled=True))


def solution(mesh):
    axes = Mesh(mesh.devices.reshape(NX, NY, NZ, NC), ("x", "y", "z", "c"))
    tokens = P(("z", "c"), ("x", "y"), None)
    weights = P(("z", "c"), None)
    return jax.shard_map(
        per_device,
        mesh=axes,
        in_specs=(tokens, weights, weights, P(), P(("z", "c"))),
        out_specs=tokens,
        check_vma=False,
    )
```

```python
import jax
import jax.numpy as jnp
from jax import lax
from jax.experimental import pallas as pl
from jax.experimental.pallas import tpu as pltpu
from jax.sharding import Mesh
from jax.sharding import PartitionSpec as P

D = 2048
H = 4
DK = 128
DV = 256
TOK = 256
NX, NY, NZ, NC = 4, 4, 16, 2
QUAD = NY * TOK
HALF = D // (NZ * NC)
PIECE = HALF + 8
EXT = DV + 128
WIDE = 2 * DK + DV + 128
lowest = -1e30


def dot(a, b, contract=((1,), (0,))):
    return lax.dot_general(a, b, (contract, ((), ())), preferred_element_type=jnp.float32)


def split3(value):
    high = value.astype(jnp.bfloat16).astype(jnp.float32)
    rest = value - high
    middle = rest.astype(jnp.bfloat16).astype(jnp.float32)
    return high, middle, rest - middle


def scan_row(row, combine, neutral):
    lane = lax.broadcasted_iota(jnp.int32, (8, 128), 1)
    sub = lax.broadcasted_iota(jnp.int32, (8, 128), 0)
    chunk = jnp.concatenate([row[:, at * 128 : at * 128 + 128] for at in range(QUAD // 128)], axis=0)
    for step in (1, 2, 4, 8, 16, 32, 64):
        chunk = combine(chunk, jnp.where(lane >= step, pltpu.roll(chunk, step, 1), neutral))
    before = jnp.broadcast_to(chunk[:, 127:], (8, 128))
    before = jnp.where(sub >= 1, pltpu.roll(before, 1, 0), neutral)
    for step in (1, 2, 4):
        before = combine(before, jnp.where(sub >= step, pltpu.roll(before, step, 0), neutral))
    chunk = combine(chunk, before)
    return jnp.concatenate([chunk[at : at + 1, :] for at in range(QUAD // 128)], axis=1)


def assemble(core, own_ref, other_ref, weight_ref):
    for part in range(4):
        for z in range(NZ):
            columns = pl.ds(part * 128, 128)
            weight_ref[z, core, :, columns] = own_ref[part, z, :HALF, :]
            weight_ref[z, 1 - core, :, columns] = other_ref[part, z, :HALF, :]
    mine = jnp.sum(own_ref[0, :, HALF:, :].astype(jnp.float32), axis=1)
    theirs = jnp.sum(other_ref[0, :, HALF:, :].astype(jnp.float32), axis=1)
    first = jnp.where(core == 0, mine, theirs)
    second = jnp.where(core == 0, theirs, mine)
    inputs = jnp.concatenate([first[:, :HALF], second[:, :HALF]], axis=1)
    forgets = jnp.concatenate([first[:, HALF:], second[:, HALF:]], axis=1)
    row = lax.broadcasted_iota(jnp.int32, (128, 128), 0)
    for z in range(NZ):
        rows = jnp.where(row == 0, inputs[z : z + 1], jnp.where(row == 1, forgets[z : z + 1], 0.0))
        columns = rows.T.astype(jnp.bfloat16).reshape(NC, HALF, 128)
        weight_ref[z, :, :, 2 * DK + DV :] = columns


def project_kernel(
    info,
    bias,
    x_hbm,
    own_ref,
    other_ref,
    q_ref,
    kt_ref,
    v_ref,
    rows_ref,
    sent_ref,
    weight_ref,
    tokens,
    arrived,
):
    copies = [
        pltpu.make_async_copy(x_hbm.at[block], tokens.at[block], arrived.at[block])
        for block in range(NY)
    ]
    for copy in copies:
        copy.start()
    assemble(info[0], own_ref, other_ref, weight_ref)
    pre = []
    for block in range(NY):
        copies[block].wait()
        here = pl.ds(block * TOK, TOK)
        projected = dot(tokens[block], weight_ref[...].reshape(D, WIDE))
        q_ref[here, :] = projected[:, :DK].astype(jnp.bfloat16)
        kt_ref[:, here] = projected[:, DK : 2 * DK].T.astype(jnp.bfloat16)
        v_ref[here, :] = projected[:, 2 * DK : 2 * DK + DV].astype(jnp.bfloat16)
        pre.append(projected[:, 2 * DK + DV :].T[:8, :])
    pre = jnp.concatenate(pre, axis=1)

    accepted = info[1]
    positions = info[2] * QUAD + lax.broadcasted_iota(jnp.int32, (1, QUAD), 1)
    live = positions < accepted
    forget_pre = pre[1:2, :] + bias[0]
    log_sigmoid = jnp.minimum(forget_pre, 0.0) - jnp.log1p(jnp.exp(-jnp.abs(forget_pre)))
    log_forget = jnp.where(live, log_sigmoid, 0.0)
    log_input = jnp.where(live, pre[0:1, :], lowest)
    decay_sum = scan_row(log_forget, jnp.add, 0.0)
    relative = log_input - decay_sum
    running_top = scan_row(relative, jnp.maximum, 2 * lowest)
    total = decay_sum[:, QUAD - 1 :]
    last_top = running_top[:, QUAD - 1 :]
    rows_ref[...] = jnp.concatenate(
        [relative, running_top, jnp.zeros((6, QUAD), jnp.float32)], axis=0
    )
    scaling = jnp.where(live, jnp.exp(relative - last_top), 0.0)
    weighted = kt_ref[...].astype(jnp.float32) * scaling
    normal = jnp.sum(weighted, axis=1, keepdims=True)
    memory = dot(weighted.astype(jnp.bfloat16), v_ref[...])
    lane = lax.broadcasted_iota(jnp.int32, (DK, 128), 1)
    logs = jnp.where(lane == 0, normal, 0.0)
    for at, value in enumerate((*split3(total), *split3(total + last_top))):
        logs = jnp.where(lane == at + 1, value, logs)
    for to in range(NX):
        sent_ref[to, :, :DV] = memory.astype(jnp.bfloat16)
        sent_ref[to, :, DV:] = logs.astype(jnp.bfloat16)


def cell_kernel(info, q_ref, kt_ref, v_ref, rows_ref, states_ref, out_ref):
    place = info[2]
    state = jnp.zeros((DK, EXT), jnp.float32)
    carry_top = jnp.full((1, 1), lowest, jnp.float32)
    for source in range(NX - 1):
        entry = states_ref[source].astype(jnp.float32)
        logs = entry[0:1, DV:]
        total = logs[:, 1:2] + (logs[:, 2:3] + logs[:, 3:4])
        top_part = logs[:, 4:5] + (logs[:, 5:6] + logs[:, 6:7])
        top_new = jnp.maximum(total + carry_top, top_part)
        joined = jnp.exp(total + carry_top - top_new) * state + jnp.exp(top_part - top_new) * entry
        state = jnp.where(source < place, joined, state)
        carry_top = jnp.where(source < place, top_new, carry_top)
    carried = state.astype(jnp.bfloat16)

    scale = DK**-0.5
    columns = rows_ref[...].T
    for block in range(NY):
        here = pl.ds(block * TOK, TOK)
        extent = (block + 1) * TOK
        top = jnp.maximum(columns[block * TOK : extent, 1:2], carry_top)
        queries = q_ref[here, :]
        scores = dot(queries, kt_ref[:, :extent]) * scale
        relative = rows_ref[0:1, :extent] - top
        row = block * TOK + lax.broadcasted_iota(jnp.int32, (TOK, extent), 0)
        column = lax.broadcasted_iota(jnp.int32, (TOK, extent), 1)
        products = jnp.exp(jnp.where(row >= column, relative, lowest)) * scores
        carry = dot(queries, carried) * (jnp.exp(carry_top - top) * scale)
        denominator = jnp.sum(products, axis=1, keepdims=True) + carry[:, DV : DV + 1]
        numerator = dot(products.astype(jnp.bfloat16), v_ref[:extent, :]) + carry[:, :DV]
        result = numerator / jnp.maximum(jnp.abs(denominator), 1.0)
        at = place * QUAD + block * TOK + lax.broadcasted_iota(jnp.int32, (TOK, 1), 0)
        out_ref[block] = jnp.where(at < info[1], result, 0.0).astype(jnp.bfloat16)


def merge_kernel(heads_ref, out_ref):
    for head in range(H):
        out_ref[0, :, head * DV : (head + 1) * DV] = heads_ref[head]


SMEM = pl.BlockSpec(memory_space=pltpu.SMEM)
VMEM = pl.BlockSpec(memory_space=pltpu.VMEM)


def granted(mebibytes):
    return pltpu.CompilerParams(vmem_limit_bytes=mebibytes * 1024 * 1024)


def shaped(*shape, dtype=jnp.bfloat16):
    return jax.ShapeDtypeStruct(shape, dtype)


def project(info, bias, quad, own, other, **options):
    return pl.pallas_call(
        project_kernel,
        out_shape=(
            shaped(QUAD, DK),
            shaped(DK, QUAD),
            shaped(QUAD, DV),
            shaped(8, QUAD, dtype=jnp.float32),
            shaped(NX, DK, EXT),
        ),
        in_specs=[SMEM, SMEM, pl.BlockSpec(memory_space=pltpu.HBM), VMEM, VMEM],
        out_specs=(VMEM,) * 5,
        scratch_shapes=[
            pltpu.VMEM((NZ, NC, HALF, WIDE), jnp.bfloat16),
            pltpu.VMEM((NY, TOK, D), jnp.bfloat16),
            pltpu.SemaphoreType.DMA((NY,)),
        ],
        compiler_params=granted(49),
        name="project",
        **options,
    )(info, bias, quad, own, other)


def cell(info, q, kt, v, rows, states, **options):
    return pl.pallas_call(
        cell_kernel,
        out_shape=shaped(NY, TOK, DV),
        in_specs=[SMEM] + [VMEM] * 5,
        out_specs=VMEM,
        compiler_params=granted(16),
        name="cell",
        **options,
    )(info, q, kt, v, rows, states)


def merge(heads, **options):
    return pl.pallas_call(
        merge_kernel,
        out_shape=shaped(1, TOK, H * DV),
        in_specs=[VMEM],
        out_specs=VMEM,
        compiler_params=granted(8),
        name="merge",
        **options,
    )(heads)


def piece_kernel(place, proj_ref, gate_ref, out_ref):
    x, y = place[0], place[1]
    for quarter, at in enumerate((y, H + y, 2 * H + 2 * y, 2 * H + 2 * y + 1)):

        @pl.when(x == quarter)
        def _(at=at):
            out_ref[0, :HALF, :] = proj_ref[:, pl.ds(pl.multiple_of(at * 128, 128), 128)]

    lane = lax.broadcasted_iota(jnp.int32, (HALF, 2 * H), 1)
    gates = gate_ref[...].astype(jnp.float32)
    inputs = jnp.sum(jnp.where(lane == y, gates, 0.0), axis=1, keepdims=True)
    forgets = jnp.sum(jnp.where(lane == H + y, gates, 0.0), axis=1, keepdims=True)
    both = jnp.broadcast_to(jnp.concatenate([inputs, forgets], axis=0), (128, 128))
    row = lax.broadcasted_iota(jnp.int32, (8, 128), 0)
    out_ref[0, HALF:, :] = jnp.where(row == 0, both.T[:8, :], 0.0).astype(jnp.bfloat16)
    for to in range(1, NZ):
        out_ref[to] = out_ref[0]


def weight_piece(place, proj_weight, gate_weight, **options):
    return pl.pallas_call(
        piece_kernel,
        out_shape=shaped(NZ, PIECE, 128),
        in_specs=[SMEM, VMEM, VMEM],
        out_specs=VMEM,
        compiler_params=granted(8),
        name="piece",
        **options,
    )(place, proj_weight, gate_weight)


def per_device(activations, proj_weight, gate_weight, forget_bias, accepted):
    x, y, core = (lax.axis_index(a) for a in ("x", "y", "c"))
    quad = lax.all_gather(activations, "y", axis=0, tiled=True)
    place = jnp.stack([x, y]).astype(jnp.int32)
    rows = lax.all_to_all(weight_piece(place, proj_weight, gate_weight), "z", 0, 0, tiled=True)
    own = lax.all_to_all(jnp.tile(rows, (NX, 1, 1)), "x", 0, 0, tiled=True)
    other = lax.ppermute(own, "c", [(0, 1), (1, 0)])
    shape = (4, NZ, PIECE, 128)
    info = jnp.stack([core, accepted[0], x]).astype(jnp.int32)
    bias = lax.dynamic_slice(forget_bias, (y,), (1,))
    q, kt, v, gates, sent = project(info, bias, quad, own.reshape(shape), other.reshape(shape))
    states = lax.all_to_all(sent, "x", 0, 0, tiled=True)
    out = cell(info, q, kt, v, gates, states)
    return merge(lax.all_to_all(out, "y", 0, 0, tiled=True))


def solution(mesh):
    axes = Mesh(mesh.devices.reshape(NX, NY, NZ, NC), ("x", "y", "z", "c"))
    tokens = P(("z", "c"), ("x", "y"), None)
    weights = P(("z", "c"), None)
    return jax.shard_map(
        per_device,
        mesh=axes,
        in_specs=(tokens, weights, weights, P(), P(("z", "c"))),
        out_specs=tokens,
        check_vma=False,
    )
```

```python
import jax
import jax.numpy as jnp
from jax import lax
from jax.experimental import pallas as pl
from jax.experimental.pallas import tpu as pltpu
from jax.sharding import Mesh
from jax.sharding import PartitionSpec as P

D = 2048
H = 4
DK = 128
DV = 256
TOK = 256
NX, NY, NZ, NC = 4, 4, 16, 2
QUAD = NY * TOK
HALF = D // (NZ * NC)
CUT = 160
PIECE = HALF + 8
EXT = DV + 128
WIDE = 2 * DK + DV + 128
lowest = -1e30


def dot(a, b, contract=((1,), (0,))):
    return lax.dot_general(a, b, (contract, ((), ())), preferred_element_type=jnp.float32)


def split3(value):
    high = value.astype(jnp.bfloat16).astype(jnp.float32)
    rest = value - high
    middle = rest.astype(jnp.bfloat16).astype(jnp.float32)
    return high, middle, rest - middle


def scan_row(row, combine, neutral):
    lane = lax.broadcasted_iota(jnp.int32, (8, 128), 1)
    sub = lax.broadcasted_iota(jnp.int32, (8, 128), 0)
    chunk = jnp.concatenate([row[:, at * 128 : at * 128 + 128] for at in range(QUAD // 128)], axis=0)
    for step in (1, 2, 4, 8, 16, 32, 64):
        chunk = combine(chunk, jnp.where(lane >= step, pltpu.roll(chunk, step, 1), neutral))
    before = jnp.broadcast_to(chunk[:, 127:], (8, 128))
    before = jnp.where(sub >= 1, pltpu.roll(before, 1, 0), neutral)
    for step in (1, 2, 4):
        before = combine(before, jnp.where(sub >= step, pltpu.roll(before, step, 0), neutral))
    chunk = combine(chunk, before)
    return jnp.concatenate([chunk[at : at + 1, :] for at in range(QUAD // 128)], axis=1)


def assemble(core, own_ref, other_ref, weight_ref):
    for part in range(4):
        for z in range(NZ):
            columns = pl.ds(part * 128, 128)
            weight_ref[z, core, :, columns] = own_ref[part, z, :HALF, :]
            weight_ref[z, 1 - core, :, columns] = other_ref[part, z, :HALF, :]
    mine = jnp.sum(own_ref[0, :, HALF:, :].astype(jnp.float32), axis=1)
    theirs = jnp.sum(other_ref[0, :, HALF:, :].astype(jnp.float32), axis=1)
    first = jnp.where(core == 0, mine, theirs)
    second = jnp.where(core == 0, theirs, mine)
    inputs = jnp.concatenate([first[:, :HALF], second[:, :HALF]], axis=1)
    forgets = jnp.concatenate([first[:, HALF:], second[:, HALF:]], axis=1)
    row = lax.broadcasted_iota(jnp.int32, (128, 128), 0)
    for z in range(NZ):
        rows = jnp.where(row == 0, inputs[z : z + 1], jnp.where(row == 1, forgets[z : z + 1], 0.0))
        columns = rows.T.astype(jnp.bfloat16).reshape(NC, HALF, 128)
        weight_ref[z, :, :, 2 * DK + DV :] = columns


def project_kernel(
    info,
    bias,
    x_ref,
    near_ref,
    far_ref,
    head_ref,
    tail_ref,
    own_ref,
    other_ref,
    q_ref,
    kt_ref,
    v_ref,
    rows_ref,
    sent_ref,
    weight_ref,
    pre_ref,
    scaling_ref,
):
    assemble(info[0], own_ref, other_ref, weight_ref)
    across = jnp.concatenate([head_ref[...], tail_ref[...]], axis=0)
    tokens = {0: x_ref[0], 1: near_ref[...], 3: far_ref[...], 2: across}
    places = {
        swap: pl.ds(pl.multiple_of(jnp.bitwise_xor(info[3], swap) * TOK, TOK), TOK)
        for swap in tokens
    }
    for swap, part in tokens.items():
        gates = dot(part, weight_ref[:, :, :, 2 * DK + DV :].reshape(D, 128))
        pre_ref[:, places[swap]] = gates.T[:8, :]

    live = info[2] * QUAD + lax.broadcasted_iota(jnp.int32, (1, QUAD), 1) < info[1]
    forget_pre = pre_ref[1:2, :] + bias[0]
    log_sigmoid = jnp.minimum(forget_pre, 0.0) - jnp.log1p(jnp.exp(-jnp.abs(forget_pre)))
    log_forget = jnp.where(live, log_sigmoid, 0.0)
    log_input = jnp.where(live, pre_ref[0:1, :], lowest)
    decay_sum = scan_row(log_forget, jnp.add, 0.0)
    relative = log_input - decay_sum
    running_top = scan_row(relative, jnp.maximum, 2 * lowest)
    total = decay_sum[:, QUAD - 1 :]
    last_top = running_top[:, QUAD - 1 :]
    rows_ref[...] = jnp.concatenate(
        [relative, running_top, jnp.zeros((6, QUAD), jnp.float32)], axis=0
    )
    scaling_ref[0:1, :] = jnp.where(live, jnp.exp(relative - last_top), 0.0)

    memory = jnp.zeros((DK, DV), jnp.float32)
    normal = jnp.zeros((DK, TOK), jnp.float32)
    for swap, part in tokens.items():
        here = places[swap]
        projected = dot(part, weight_ref[:, :, :, : 2 * DK + DV].reshape(D, 2 * DK + DV))
        keys = projected[:, DK : 2 * DK].astype(jnp.bfloat16).T
        values = projected[:, 2 * DK :].astype(jnp.bfloat16)
        q_ref[here, :] = projected[:, :DK].astype(jnp.bfloat16)
        kt_ref[:, here] = keys
        v_ref[here, :] = values
        weighted = keys.astype(jnp.float32) * scaling_ref[0:1, here]
        normal = normal + weighted
        memory = memory + dot(weighted.astype(jnp.bfloat16), values)
    normal = jnp.sum(normal, axis=1, keepdims=True)
    lane = lax.broadcasted_iota(jnp.int32, (DK, 128), 1)
    logs = jnp.where(lane == 0, normal, 0.0)
    for at, value in enumerate((*split3(total), *split3(total + last_top))):
        logs = jnp.where(lane == at + 1, value, logs)
    for to in range(NX):
        sent_ref[to, :, :DV] = memory.astype(jnp.bfloat16)
        sent_ref[to, :, DV:] = logs.astype(jnp.bfloat16)


def cell_kernel(info, q_ref, kt_ref, v_ref, rows_ref, states_ref, out_ref):
    place = info[2]
    state = jnp.zeros((DK, EXT), jnp.float32)
    carry_top = jnp.full((1, 1), lowest, jnp.float32)
    for source in range(NX - 1):
        entry = states_ref[source].astype(jnp.float32)
        logs = entry[0:1, DV:]
        total = logs[:, 1:2] + (logs[:, 2:3] + logs[:, 3:4])
        top_part = logs[:, 4:5] + (logs[:, 5:6] + logs[:, 6:7])
        top_new = jnp.maximum(total + carry_top, top_part)
        joined = jnp.exp(total + carry_top - top_new) * state + jnp.exp(top_part - top_new) * entry
        state = jnp.where(source < place, joined, state)
        carry_top = jnp.where(source < place, top_new, carry_top)
    carried = state.astype(jnp.bfloat16)

    scale = DK**-0.5
    columns = rows_ref[...].T
    for block in range(NY):
        here = pl.ds(block * TOK, TOK)
        extent = (block + 1) * TOK
        top = jnp.maximum(columns[block * TOK : extent, 1:2], carry_top)
        queries = q_ref[here, :]
        scores = dot(queries, kt_ref[:, :extent]) * scale
        relative = rows_ref[0:1, :extent] - top
        row = block * TOK + lax.broadcasted_iota(jnp.int32, (TOK, extent), 0)
        column = lax.broadcasted_iota(jnp.int32, (TOK, extent), 1)
        products = jnp.exp(jnp.where(row >= column, relative, lowest)) * scores
        carry = dot(queries, carried) * (jnp.exp(carry_top - top) * scale)
        denominator = jnp.sum(products, axis=1, keepdims=True) + carry[:, DV : DV + 1]
        numerator = dot(products.astype(jnp.bfloat16), v_ref[:extent, :]) + carry[:, :DV]
        result = numerator / jnp.maximum(jnp.abs(denominator), 1.0)
        at = place * QUAD + block * TOK + lax.broadcasted_iota(jnp.int32, (TOK, 1), 0)
        out_ref[block] = jnp.where(at < info[1], result, 0.0).astype(jnp.bfloat16)


def merge_kernel(heads_ref, out_ref):
    for head in range(H):
        out_ref[0, :, head * DV : (head + 1) * DV] = heads_ref[head]


SMEM = pl.BlockSpec(memory_space=pltpu.SMEM)
VMEM = pl.BlockSpec(memory_space=pltpu.VMEM)


def granted(mebibytes):
    return pltpu.CompilerParams(vmem_limit_bytes=mebibytes * 1024 * 1024)


def shaped(*shape, dtype=jnp.bfloat16):
    return jax.ShapeDtypeStruct(shape, dtype)


def project(info, bias, tokens, own, other, **options):
    return pl.pallas_call(
        project_kernel,
        out_shape=(
            shaped(QUAD, DK),
            shaped(DK, QUAD),
            shaped(QUAD, DV),
            shaped(8, QUAD, dtype=jnp.float32),
            shaped(NX, DK, EXT),
        ),
        in_specs=[SMEM, SMEM] + [VMEM] * 7,
        out_specs=(VMEM,) * 5,
        scratch_shapes=[
            pltpu.VMEM((NZ, NC, HALF, WIDE), jnp.bfloat16),
            pltpu.VMEM((8, QUAD), jnp.float32),
            pltpu.VMEM((8, QUAD), jnp.float32),
        ],
        compiler_params=granted(24),
        name="project",
        **options,
    )(info, bias, *tokens, own, other)


def cell(info, q, kt, v, rows, states, **options):
    return pl.pallas_call(
        cell_kernel,
        out_shape=shaped(NY, TOK, DV),
        in_specs=[SMEM] + [VMEM] * 5,
        out_specs=VMEM,
        compiler_params=granted(16),
        name="cell",
        **options,
    )(info, q, kt, v, rows, states)


def merge(heads, **options):
    return pl.pallas_call(
        merge_kernel,
        out_shape=shaped(1, TOK, H * DV),
        in_specs=[VMEM],
        out_specs=VMEM,
        compiler_params=granted(8),
        name="merge",
        **options,
    )(heads)


def piece_kernel(place, proj_ref, gate_ref, out_ref):
    x, y = place[0], place[1]
    for quarter, at in enumerate((y, H + y, 2 * H + 2 * y, 2 * H + 2 * y + 1)):

        @pl.when(x == quarter)
        def _(at=at):
            out_ref[0, :HALF, :] = proj_ref[:, pl.ds(pl.multiple_of(at * 128, 128), 128)]

    lane = lax.broadcasted_iota(jnp.int32, (HALF, 2 * H), 1)
    gates = gate_ref[...].astype(jnp.float32)
    inputs = jnp.sum(jnp.where(lane == y, gates, 0.0), axis=1, keepdims=True)
    forgets = jnp.sum(jnp.where(lane == H + y, gates, 0.0), axis=1, keepdims=True)
    both = jnp.broadcast_to(jnp.concatenate([inputs, forgets], axis=0), (128, 128))
    row = lax.broadcasted_iota(jnp.int32, (8, 128), 0)
    out_ref[0, HALF:, :] = jnp.where(row == 0, both.T[:8, :], 0.0).astype(jnp.bfloat16)
    for to in range(1, NZ):
        out_ref[to] = out_ref[0]


def weight_piece(place, proj_weight, gate_weight, **options):
    return pl.pallas_call(
        piece_kernel,
        out_shape=shaped(NZ, PIECE, 128),
        in_specs=[SMEM, VMEM, VMEM],
        out_specs=VMEM,
        compiler_params=granted(8),
        name="piece",
        **options,
    )(place, proj_weight, gate_weight)


def swap_along(array, axis, swap):
    return lax.ppermute(array, axis, [(i, i ^ swap) for i in range(4)])


def per_device(activations, proj_weight, gate_weight, forget_bias, accepted):
    x, y, core = (lax.axis_index(a) for a in ("x", "y", "c"))
    own_tokens = activations[0]
    near = swap_along(own_tokens, "y", 1)
    far = swap_along(own_tokens, "y", 3)
    head = swap_along(near[:CUT], "y", 3)
    tail = swap_along(far[CUT:], "y", 1)
    place = jnp.stack([x, y]).astype(jnp.int32)
    rows = lax.all_to_all(weight_piece(place, proj_weight, gate_weight), "z", 0, 0)
    own = lax.all_to_all(jnp.tile(rows.reshape(1, NZ * PIECE, 128), (NX, 1, 1)), "x", 0, 0)
    own, head, tail = lax.optimization_barrier((own.reshape(NX * NZ * PIECE, 128), head, tail))
    other = lax.ppermute(own, "c", [(0, 1), (1, 0)])
    shape = (4, NZ, PIECE, 128)
    info = jnp.stack([core, accepted[0], x, y]).astype(jnp.int32)
    bias = lax.dynamic_slice(forget_bias, (y,), (1,))
    tokens = (activations, near, far, head, tail)
    q, kt, v, gates, sent = project(info, bias, tokens, own.reshape(shape), other.reshape(shape))
    states = lax.all_to_all(sent, "x", 0, 0, tiled=True)
    out = cell(info, q, kt, v, gates, states)
    return merge(lax.all_to_all(out, "y", 0, 0, tiled=True))


def solution(mesh):
    axes = Mesh(mesh.devices.reshape(NX, NY, NZ, NC), ("x", "y", "z", "c"))
    tokens = P(("z", "c"), ("x", "y"), None)
    weights = P(("z", "c"), None)
    return jax.shard_map(
        per_device,
        mesh=axes,
        in_specs=(tokens, weights, weights, P(), P(("z", "c"))),
        out_specs=tokens,
        check_vma=False,
    )
```

```python
import jax
import jax.numpy as jnp
from jax import lax
from jax.experimental import pallas as pl
from jax.experimental.pallas import tpu as pltpu
from jax.sharding import Mesh
from jax.sharding import PartitionSpec as P

D = 2048
H = 4
DK = 128
DV = 256
TOK = 256
NX, NY, NZ, NC = 4, 4, 16, 2
QUAD = NY * TOK
HALF = D // (NZ * NC)
CUT = 160
PIECE = HALF + 8
EXT = DV + 128
WIDE = 2 * DK + DV + 128
lowest = -1e30


def dot(a, b, contract=((1,), (0,))):
    return lax.dot_general(a, b, (contract, ((), ())), preferred_element_type=jnp.float32)


def split3(value):
    high = value.astype(jnp.bfloat16).astype(jnp.float32)
    rest = value - high
    middle = rest.astype(jnp.bfloat16).astype(jnp.float32)
    return high, middle, rest - middle


def scan_row(row, combine, neutral):
    lane = lax.broadcasted_iota(jnp.int32, (8, 128), 1)
    sub = lax.broadcasted_iota(jnp.int32, (8, 128), 0)
    chunk = jnp.concatenate([row[:, at * 128 : at * 128 + 128] for at in range(QUAD // 128)], axis=0)
    for step in (1, 2, 4, 8, 16, 32, 64):
        chunk = combine(chunk, jnp.where(lane >= step, pltpu.roll(chunk, step, 1), neutral))
    before = jnp.broadcast_to(chunk[:, 127:], (8, 128))
    before = jnp.where(sub >= 1, pltpu.roll(before, 1, 0), neutral)
    for step in (1, 2, 4):
        before = combine(before, jnp.where(sub >= step, pltpu.roll(before, step, 0), neutral))
    chunk = combine(chunk, before)
    return jnp.concatenate([chunk[at : at + 1, :] for at in range(QUAD // 128)], axis=1)


def assemble(core, own_ref, other_ref, weight_ref):
    for part in range(4):
        for z in range(NZ):
            columns = pl.ds(part * 128, 128)
            weight_ref[z, core, :, columns] = own_ref[part, z, :HALF, :]
            weight_ref[z, 1 - core, :, columns] = other_ref[part, z, :HALF, :]
    mine = jnp.sum(own_ref[0, :, HALF:, :].astype(jnp.float32), axis=1)
    theirs = jnp.sum(other_ref[0, :, HALF:, :].astype(jnp.float32), axis=1)
    first = jnp.where(core == 0, mine, theirs)
    second = jnp.where(core == 0, theirs, mine)
    inputs = jnp.concatenate([first[:, :HALF], second[:, :HALF]], axis=1)
    forgets = jnp.concatenate([first[:, HALF:], second[:, HALF:]], axis=1)
    row = lax.broadcasted_iota(jnp.int32, (128, 128), 0)
    for z in range(NZ):
        rows = jnp.where(row == 0, inputs[z : z + 1], jnp.where(row == 1, forgets[z : z + 1], 0.0))
        columns = rows.T.astype(jnp.bfloat16).reshape(NC, HALF, 128)
        weight_ref[z, :, :, 2 * DK + DV :] = columns


def project_kernel(
    info,
    bias,
    x_ref,
    near_ref,
    far_ref,
    head_ref,
    tail_ref,
    own_ref,
    other_ref,
    q_ref,
    kt_ref,
    v_ref,
    rows_ref,
    sent_ref,
    weight_ref,
    pre_ref,
    scaling_ref,
):
    assemble(info[0], own_ref, other_ref, weight_ref)
    across = jnp.concatenate([head_ref[...], tail_ref[...]], axis=0)
    tokens = {0: x_ref[0], 1: near_ref[...], 3: far_ref[...], 2: across}
    places = {
        swap: pl.ds(pl.multiple_of(jnp.bitwise_xor(info[3], swap) * TOK, TOK), TOK)
        for swap in tokens
    }
    for swap, part in tokens.items():
        gates = dot(part, weight_ref[:, :, :, 2 * DK + DV :].reshape(D, 128))
        pre_ref[:, places[swap]] = gates.T[:8, :]

    live = info[2] * QUAD + lax.broadcasted_iota(jnp.int32, (1, QUAD), 1) < info[1]
    forget_pre = pre_ref[1:2, :] + bias[0]
    log_sigmoid = jnp.minimum(forget_pre, 0.0) - jnp.log1p(jnp.exp(-jnp.abs(forget_pre)))
    log_forget = jnp.where(live, log_sigmoid, 0.0)
    log_input = jnp.where(live, pre_ref[0:1, :], lowest)
    decay_sum = scan_row(log_forget, jnp.add, 0.0)
    relative = log_input - decay_sum
    running_top = scan_row(relative, jnp.maximum, 2 * lowest)
    total = decay_sum[:, QUAD - 1 :]
    last_top = running_top[:, QUAD - 1 :]
    rows_ref[...] = jnp.concatenate(
        [relative, running_top, jnp.zeros((6, QUAD), jnp.float32)], axis=0
    )
    scaling_ref[0:1, :] = jnp.where(live, jnp.exp(relative - last_top), 0.0)

    memory = jnp.zeros((DK, DV), jnp.float32)
    normal = jnp.zeros((DK, TOK), jnp.float32)
    for swap, part in tokens.items():
        here = places[swap]
        projected = dot(part, weight_ref[:, :, :, : 2 * DK + DV].reshape(D, 2 * DK + DV))
        keys = projected[:, DK : 2 * DK].astype(jnp.bfloat16).T
        values = projected[:, 2 * DK :].astype(jnp.bfloat16)
        q_ref[here, :] = projected[:, :DK].astype(jnp.bfloat16)
        kt_ref[:, here] = keys
        v_ref[here, :] = values
        weighted = keys.astype(jnp.float32) * scaling_ref[0:1, here]
        normal = normal + weighted
        memory = memory + dot(weighted.astype(jnp.bfloat16), values)
    normal = jnp.sum(normal, axis=1, keepdims=True)
    lane = lax.broadcasted_iota(jnp.int32, (DK, 128), 1)
    logs = jnp.where(lane == 0, normal, 0.0)
    for at, value in enumerate((*split3(total), *split3(total + last_top))):
        logs = jnp.where(lane == at + 1, value, logs)
    for to in range(NX):
        sent_ref[to, :, :DV] = memory.astype(jnp.bfloat16)
        sent_ref[to, :, DV:] = logs.astype(jnp.bfloat16)


def cell_kernel(info, q_ref, kt_ref, v_ref, rows_ref, states_ref, out_ref):
    place = info[2]
    state = jnp.zeros((DK, EXT), jnp.float32)
    carry_top = jnp.full((1, 1), lowest, jnp.float32)
    for source in range(NX - 1):
        entry = states_ref[source].astype(jnp.float32)
        logs = entry[0:1, DV:]
        total = logs[:, 1:2] + (logs[:, 2:3] + logs[:, 3:4])
        top_part = logs[:, 4:5] + (logs[:, 5:6] + logs[:, 6:7])
        top_new = jnp.maximum(total + carry_top, top_part)
        joined = jnp.exp(total + carry_top - top_new) * state + jnp.exp(top_part - top_new) * entry
        state = jnp.where(source < place, joined, state)
        carry_top = jnp.where(source < place, top_new, carry_top)
    carried = state.astype(jnp.bfloat16)

    scale = DK**-0.5
    columns = rows_ref[...].T
    for block in range(NY):
        here = pl.ds(block * TOK, TOK)
        extent = (block + 1) * TOK
        top = jnp.maximum(columns[block * TOK : extent, 1:2], carry_top)
        queries = q_ref[here, :]
        scores = dot(queries, kt_ref[:, :extent]) * scale
        relative = rows_ref[0:1, :extent] - top
        row = block * TOK + lax.broadcasted_iota(jnp.int32, (TOK, extent), 0)
        column = lax.broadcasted_iota(jnp.int32, (TOK, extent), 1)
        products = jnp.exp(jnp.where(row >= column, relative, lowest)) * scores
        carry = dot(queries, carried) * (jnp.exp(carry_top - top) * scale)
        denominator = jnp.sum(products, axis=1, keepdims=True) + carry[:, DV : DV + 1]
        numerator = dot(products.astype(jnp.bfloat16), v_ref[:extent, :]) + carry[:, :DV]
        result = numerator / jnp.maximum(jnp.abs(denominator), 1.0)
        at = place * QUAD + block * TOK + lax.broadcasted_iota(jnp.int32, (TOK, 1), 0)
        out_ref[block] = jnp.where(at < info[1], result, 0.0).astype(jnp.bfloat16)


def merge_kernel(heads_ref, out_ref):
    for head in range(H):
        out_ref[0, :, head * DV : (head + 1) * DV] = heads_ref[head]


SMEM = pl.BlockSpec(memory_space=pltpu.SMEM)
VMEM = pl.BlockSpec(memory_space=pltpu.VMEM)


def granted(mebibytes):
    return pltpu.CompilerParams(vmem_limit_bytes=mebibytes * 1024 * 1024)


def shaped(*shape, dtype=jnp.bfloat16):
    return jax.ShapeDtypeStruct(shape, dtype)


def project(info, bias, tokens, own, other, **options):
    return pl.pallas_call(
        project_kernel,
        out_shape=(
            shaped(QUAD, DK),
            shaped(DK, QUAD),
            shaped(QUAD, DV),
            shaped(8, QUAD, dtype=jnp.float32),
            shaped(NX, DK, EXT),
        ),
        in_specs=[SMEM, SMEM] + [VMEM] * 7,
        out_specs=(VMEM,) * 5,
        scratch_shapes=[
            pltpu.VMEM((NZ, NC, HALF, WIDE), jnp.bfloat16),
            pltpu.VMEM((8, QUAD), jnp.float32),
            pltpu.VMEM((8, QUAD), jnp.float32),
        ],
        compiler_params=granted(48),
        name="project",
        **options,
    )(info, bias, *tokens, own, other)


def cell(info, q, kt, v, rows, states, **options):
    return pl.pallas_call(
        cell_kernel,
        out_shape=shaped(NY, TOK, DV),
        in_specs=[SMEM] + [VMEM] * 5,
        out_specs=VMEM,
        compiler_params=granted(16),
        name="cell",
        **options,
    )(info, q, kt, v, rows, states)


def merge(heads, **options):
    return pl.pallas_call(
        merge_kernel,
        out_shape=shaped(1, TOK, H * DV),
        in_specs=[VMEM],
        out_specs=VMEM,
        compiler_params=granted(8),
        name="merge",
        **options,
    )(heads)


def piece_kernel(place, proj_ref, gate_ref, out_ref):
    x, y = place[0], place[1]
    for quarter, at in enumerate((y, H + y, 2 * H + 2 * y, 2 * H + 2 * y + 1)):

        @pl.when(x == quarter)
        def _(at=at):
            out_ref[0, :HALF, :] = proj_ref[:, pl.ds(pl.multiple_of(at * 128, 128), 128)]

    gates = gate_ref[...].astype(jnp.float32)
    column = lax.broadcasted_iota(jnp.int32, (2 * H, HALF), 0)
    inputs = jnp.sum(jnp.where(column == y, gates, 0.0), axis=0, keepdims=True)
    forgets = jnp.sum(jnp.where(column == H + y, gates, 0.0), axis=0, keepdims=True)
    both = jnp.concatenate([inputs, forgets], axis=1)
    row = lax.broadcasted_iota(jnp.int32, (8, 128), 0)
    out_ref[0, HALF:, :] = jnp.where(row == 0, both, 0.0).astype(jnp.bfloat16)
    for to in range(1, NZ):
        out_ref[to] = out_ref[0]


def weight_piece(place, proj_weight, gate_weight, **options):
    return pl.pallas_call(
        piece_kernel,
        out_shape=shaped(NZ, PIECE, 128),
        in_specs=[SMEM, VMEM, VMEM],
        out_specs=VMEM,
        compiler_params=granted(8),
        name="piece",
        **options,
    )(place, proj_weight, gate_weight.T)


def swap_along(array, axis, swap):
    return lax.ppermute(array, axis, [(i, i ^ swap) for i in range(4)])


def per_device(activations, proj_weight, gate_weight, forget_bias, accepted):
    x, y, core = (lax.axis_index(a) for a in ("x", "y", "c"))
    own_tokens = activations[0]
    near = swap_along(own_tokens, "y", 1)
    far = swap_along(own_tokens, "y", 3)
    head = swap_along(near[:CUT], "y", 3)
    tail = swap_along(far[CUT:], "y", 1)
    place = jnp.stack([x, y]).astype(jnp.int32)
    rows = lax.all_to_all(weight_piece(place, proj_weight, gate_weight), "z", 0, 0)
    own = lax.all_to_all(jnp.tile(rows.reshape(1, NZ * PIECE, 128), (NX, 1, 1)), "x", 0, 0)
    own, head, tail = lax.optimization_barrier((own.reshape(NX * NZ * PIECE, 128), head, tail))
    other = lax.ppermute(own, "c", [(0, 1), (1, 0)])
    shape = (4, NZ, PIECE, 128)
    info = jnp.stack([core, accepted[0], x, y]).astype(jnp.int32)
    bias = lax.dynamic_slice(forget_bias, (y,), (1,))
    tokens = (activations, near, far, head, tail)
    q, kt, v, gates, sent = project(info, bias, tokens, own.reshape(shape), other.reshape(shape))
    states = lax.all_to_all(sent, "x", 0, 0, tiled=True)
    out = cell(info, q, kt, v, gates, states)
    return merge(lax.all_to_all(out, "y", 0, 0, tiled=True))


def solution(mesh):
    axes = Mesh(mesh.devices.reshape(NX, NY, NZ, NC), ("x", "y", "z", "c"))
    tokens = P(("z", "c"), ("x", "y"), None)
    weights = P(("z", "c"), None)
    return jax.shard_map(
        per_device,
        mesh=axes,
        in_specs=(tokens, weights, weights, P(), P(("z", "c"))),
        out_specs=tokens,
        check_vma=False,
    )
```

```python
import jax
import jax.numpy as jnp
from jax import lax
from jax.experimental import pallas as pl
from jax.experimental.pallas import tpu as pltpu
from jax.sharding import Mesh
from jax.sharding import PartitionSpec as P

D = 2048
H = 4
DK = 128
DV = 256
TOK = 256
NX, NY, NZ, NC = 4, 4, 16, 2
QUAD = NY * TOK
HALF = D // (NZ * NC)
CUT = 144
PIECE = HALF + 8
EXT = DV + 128
WIDE = 2 * DK + DV + 128
lowest = -1e30


def dot(a, b, contract=((1,), (0,))):
    return lax.dot_general(a, b, (contract, ((), ())), preferred_element_type=jnp.float32)


def split3(value):
    high = value.astype(jnp.bfloat16).astype(jnp.float32)
    rest = value - high
    middle = rest.astype(jnp.bfloat16).astype(jnp.float32)
    return high, middle, rest - middle


def scan_row(row, combine, neutral):
    lane = lax.broadcasted_iota(jnp.int32, (8, 128), 1)
    sub = lax.broadcasted_iota(jnp.int32, (8, 128), 0)
    chunk = jnp.concatenate([row[:, at * 128 : at * 128 + 128] for at in range(QUAD // 128)], axis=0)
    for step in (1, 2, 4, 8, 16, 32, 64):
        chunk = combine(chunk, jnp.where(lane >= step, pltpu.roll(chunk, step, 1), neutral))
    before = jnp.broadcast_to(chunk[:, 127:], (8, 128))
    before = jnp.where(sub >= 1, pltpu.roll(before, 1, 0), neutral)
    for step in (1, 2, 4):
        before = combine(before, jnp.where(sub >= step, pltpu.roll(before, step, 0), neutral))
    chunk = combine(chunk, before)
    return jnp.concatenate([chunk[at : at + 1, :] for at in range(QUAD // 128)], axis=1)


def assemble(core, own_ref, other_ref, weight_ref):
    for part in range(4):
        for z in range(NZ):
            columns = pl.ds(part * 128, 128)
            weight_ref[z, core, :, columns] = own_ref[part, z, :HALF, :]
            weight_ref[z, 1 - core, :, columns] = other_ref[part, z, :HALF, :]
    mine = jnp.sum(own_ref[0, :, HALF:, :].astype(jnp.float32), axis=1)
    theirs = jnp.sum(other_ref[0, :, HALF:, :].astype(jnp.float32), axis=1)
    first = jnp.where(core == 0, mine, theirs)
    second = jnp.where(core == 0, theirs, mine)
    inputs = jnp.concatenate([first[:, :HALF], second[:, :HALF]], axis=1)
    forgets = jnp.concatenate([first[:, HALF:], second[:, HALF:]], axis=1)
    row = lax.broadcasted_iota(jnp.int32, (128, 128), 0)
    for z in range(NZ):
        rows = jnp.where(row == 0, inputs[z : z + 1], jnp.where(row == 1, forgets[z : z + 1], 0.0))
        columns = rows.T.astype(jnp.bfloat16).reshape(NC, HALF, 128)
        weight_ref[z, :, :, 2 * DK + DV :] = columns


def project_kernel(
    info,
    bias,
    x_ref,
    near_ref,
    far_ref,
    head_ref,
    tail_ref,
    own_ref,
    other_ref,
    q_ref,
    kt_ref,
    v_ref,
    rows_ref,
    sent_ref,
    weight_ref,
    pre_ref,
    scaling_ref,
):
    assemble(info[0], own_ref, other_ref, weight_ref)
    across = jnp.concatenate([head_ref[...], tail_ref[...]], axis=0)
    tokens = {0: x_ref[0], 1: near_ref[...], 3: far_ref[...], 2: across}
    places = {
        swap: pl.ds(pl.multiple_of(jnp.bitwise_xor(info[3], swap) * TOK, TOK), TOK)
        for swap in tokens
    }
    for swap, part in tokens.items():
        gates = dot(part, weight_ref[:, :, :, 2 * DK + DV :].reshape(D, 128))
        pre_ref[:, places[swap]] = gates.T[:8, :]

    live = info[2] * QUAD + lax.broadcasted_iota(jnp.int32, (1, QUAD), 1) < info[1]
    forget_pre = pre_ref[1:2, :] + bias[0]
    log_sigmoid = jnp.minimum(forget_pre, 0.0) - jnp.log1p(jnp.exp(-jnp.abs(forget_pre)))
    log_forget = jnp.where(live, log_sigmoid, 0.0)
    log_input = jnp.where(live, pre_ref[0:1, :], lowest)
    decay_sum = scan_row(log_forget, jnp.add, 0.0)
    relative = log_input - decay_sum
    running_top = scan_row(relative, jnp.maximum, 2 * lowest)
    total = decay_sum[:, QUAD - 1 :]
    last_top = running_top[:, QUAD - 1 :]
    rows_ref[...] = jnp.concatenate(
        [relative, running_top, jnp.zeros((6, QUAD), jnp.float32)], axis=0
    )
    scaling_ref[0:1, :] = jnp.where(live, jnp.exp(relative - last_top), 0.0)

    memory = jnp.zeros((DK, DV), jnp.float32)
    normal = jnp.zeros((DK, TOK), jnp.float32)
    for swap, part in tokens.items():
        here = places[swap]
        projected = dot(part, weight_ref[:, :, :, : 2 * DK + DV].reshape(D, 2 * DK + DV))
        keys = projected[:, DK : 2 * DK].astype(jnp.bfloat16).T
        values = projected[:, 2 * DK :].astype(jnp.bfloat16)
        q_ref[here, :] = projected[:, :DK].astype(jnp.bfloat16)
        kt_ref[:, here] = keys
        v_ref[here, :] = values
        weighted = keys.astype(jnp.float32) * scaling_ref[0:1, here]
        normal = normal + weighted
        memory = memory + dot(weighted.astype(jnp.bfloat16), values)
    normal = jnp.sum(normal, axis=1, keepdims=True)
    lane = lax.broadcasted_iota(jnp.int32, (DK, 128), 1)
    logs = jnp.where(lane == 0, normal, 0.0)
    for at, value in enumerate((*split3(total), *split3(total + last_top))):
        logs = jnp.where(lane == at + 1, value, logs)
    for to in range(NX):
        sent_ref[to, :, :DV] = memory.astype(jnp.bfloat16)
        sent_ref[to, :, DV:] = logs.astype(jnp.bfloat16)


def cell_kernel(info, q_ref, kt_ref, v_ref, rows_ref, states_ref, out_ref):
    place = info[2]
    state = jnp.zeros((DK, EXT), jnp.float32)
    carry_top = jnp.full((1, 1), lowest, jnp.float32)
    for source in range(NX - 1):
        entry = states_ref[source].astype(jnp.float32)
        logs = entry[0:1, DV:]
        total = logs[:, 1:2] + (logs[:, 2:3] + logs[:, 3:4])
        top_part = logs[:, 4:5] + (logs[:, 5:6] + logs[:, 6:7])
        top_new = jnp.maximum(total + carry_top, top_part)
        joined = jnp.exp(total + carry_top - top_new) * state + jnp.exp(top_part - top_new) * entry
        state = jnp.where(source < place, joined, state)
        carry_top = jnp.where(source < place, top_new, carry_top)
    carried = state.astype(jnp.bfloat16)

    scale = DK**-0.5
    columns = rows_ref[...].T
    for block in range(NY):
        here = pl.ds(block * TOK, TOK)
        extent = (block + 1) * TOK
        top = jnp.maximum(columns[block * TOK : extent, 1:2], carry_top)
        queries = q_ref[here, :]
        scores = dot(queries, kt_ref[:, :extent]) * scale
        relative = rows_ref[0:1, :extent] - top
        row = block * TOK + lax.broadcasted_iota(jnp.int32, (TOK, extent), 0)
        column = lax.broadcasted_iota(jnp.int32, (TOK, extent), 1)
        products = jnp.exp(jnp.where(row >= column, relative, lowest)) * scores
        carry = dot(queries, carried) * (jnp.exp(carry_top - top) * scale)
        denominator = jnp.sum(products, axis=1, keepdims=True) + carry[:, DV : DV + 1]
        numerator = dot(products.astype(jnp.bfloat16), v_ref[:extent, :]) + carry[:, :DV]
        result = numerator / jnp.maximum(jnp.abs(denominator), 1.0)
        at = place * QUAD + block * TOK + lax.broadcasted_iota(jnp.int32, (TOK, 1), 0)
        out_ref[block] = jnp.where(at < info[1], result, 0.0).astype(jnp.bfloat16)


def merge_kernel(heads_ref, out_ref):
    for head in range(H):
        out_ref[0, :, head * DV : (head + 1) * DV] = heads_ref[head]


SMEM = pl.BlockSpec(memory_space=pltpu.SMEM)
VMEM = pl.BlockSpec(memory_space=pltpu.VMEM)


def granted(mebibytes):
    return pltpu.CompilerParams(vmem_limit_bytes=mebibytes * 1024 * 1024)


def shaped(*shape, dtype=jnp.bfloat16):
    return jax.ShapeDtypeStruct(shape, dtype)


def project(info, bias, tokens, own, other, **options):
    return pl.pallas_call(
        project_kernel,
        out_shape=(
            shaped(QUAD, DK),
            shaped(DK, QUAD),
            shaped(QUAD, DV),
            shaped(8, QUAD, dtype=jnp.float32),
            shaped(NX, DK, EXT),
        ),
        in_specs=[SMEM, SMEM] + [VMEM] * 7,
        out_specs=(VMEM,) * 5,
        scratch_shapes=[
            pltpu.VMEM((NZ, NC, HALF, WIDE), jnp.bfloat16),
            pltpu.VMEM((8, QUAD), jnp.float32),
            pltpu.VMEM((8, QUAD), jnp.float32),
        ],
        compiler_params=granted(49),
        name="project",
        **options,
    )(info, bias, *tokens, own, other)


def cell(info, q, kt, v, rows, states, **options):
    return pl.pallas_call(
        cell_kernel,
        out_shape=shaped(NY, TOK, DV),
        in_specs=[SMEM] + [VMEM] * 5,
        out_specs=VMEM,
        compiler_params=granted(16),
        name="cell",
        **options,
    )(info, q, kt, v, rows, states)


def merge(heads, **options):
    return pl.pallas_call(
        merge_kernel,
        out_shape=shaped(1, TOK, H * DV),
        in_specs=[VMEM],
        out_specs=VMEM,
        compiler_params=granted(8),
        name="merge",
        **options,
    )(heads)


def piece_kernel(place, proj_ref, gate_ref, out_ref):
    x, y = place[0], place[1]
    for quarter, at in enumerate((y, H + y, 2 * H + 2 * y, 2 * H + 2 * y + 1)):

        @pl.when(x == quarter)
        def _(at=at):
            out_ref[0, :HALF, :] = proj_ref[:, pl.ds(pl.multiple_of(at * 128, 128), 128)]

    gates = gate_ref[...].astype(jnp.float32)
    column = lax.broadcasted_iota(jnp.int32, (2 * H, HALF), 0)
    inputs = jnp.sum(jnp.where(column == y, gates, 0.0), axis=0, keepdims=True)
    forgets = jnp.sum(jnp.where(column == H + y, gates, 0.0), axis=0, keepdims=True)
    both = jnp.concatenate([inputs, forgets], axis=1)
    row = lax.broadcasted_iota(jnp.int32, (8, 128), 0)
    out_ref[0, HALF:, :] = jnp.where(row == 0, both, 0.0).astype(jnp.bfloat16)
    for to in range(1, NZ):
        out_ref[to] = out_ref[0]


def weight_piece(place, proj_weight, gate_weight, **options):
    return pl.pallas_call(
        piece_kernel,
        out_shape=shaped(NZ, PIECE, 128),
        in_specs=[SMEM, VMEM, VMEM],
        out_specs=VMEM,
        compiler_params=granted(8),
        name="piece",
        **options,
    )(place, proj_weight, gate_weight.T)


def swap_along(array, axis, swap):
    return lax.ppermute(array, axis, [(i, i ^ swap) for i in range(4)])


def per_device(activations, proj_weight, gate_weight, forget_bias, accepted):
    x, y, core = (lax.axis_index(a) for a in ("x", "y", "c"))
    own_tokens = activations[0]
    near = swap_along(own_tokens, "y", 1)
    far = swap_along(own_tokens, "y", 3)
    head = swap_along(near[:CUT], "y", 3)
    tail = swap_along(far[CUT:], "y", 1)
    place = jnp.stack([x, y]).astype(jnp.int32)
    rows = lax.all_to_all(weight_piece(place, proj_weight, gate_weight), "z", 0, 0)
    own = lax.all_to_all(jnp.tile(rows.reshape(1, NZ * PIECE, 128), (NX, 1, 1)), "x", 0, 0)
    own, head, tail = lax.optimization_barrier((own.reshape(NX * NZ * PIECE, 128), head, tail))
    other = lax.ppermute(own, "c", [(0, 1), (1, 0)])
    shape = (4, NZ, PIECE, 128)
    info = jnp.stack([core, accepted[0], x, y]).astype(jnp.int32)
    bias = lax.dynamic_slice(forget_bias, (y,), (1,))
    tokens = (activations, near, far, head, tail)
    q, kt, v, gates, sent = project(info, bias, tokens, own.reshape(shape), other.reshape(shape))
    states = lax.all_to_all(sent, "x", 0, 0, tiled=True)
    out = cell(info, q, kt, v, gates, states)
    return merge(lax.all_to_all(out, "y", 0, 0, tiled=True))


def solution(mesh):
    axes = Mesh(mesh.devices.reshape(NX, NY, NZ, NC), ("x", "y", "z", "c"))
    tokens = P(("z", "c"), ("x", "y"), None)
    weights = P(("z", "c"), None)
    return jax.shard_map(
        per_device,
        mesh=axes,
        in_specs=(tokens, weights, weights, P(), P(("z", "c"))),
        out_specs=tokens,
        check_vma=False,
    )
```

```python
import jax
import jax.numpy as jnp
from jax import lax
from jax.experimental import pallas as pl
from jax.experimental.pallas import tpu as pltpu
from jax.sharding import Mesh
from jax.sharding import PartitionSpec as P

D = 2048
H = 4
DK = 128
DV = 256
TOK = 256
NX, NY, NZ, NC = 4, 4, 16, 2
QUAD = NY * TOK
HALF = D // (NZ * NC)
CUT = 160
PIECE = HALF + 8
EXT = DV + 128
WIDE = 2 * DK + DV + 128
lowest = -1e30


def dot(a, b, contract=((1,), (0,))):
    return lax.dot_general(a, b, (contract, ((), ())), preferred_element_type=jnp.float32)


def split3(value):
    high = value.astype(jnp.bfloat16).astype(jnp.float32)
    rest = value - high
    middle = rest.astype(jnp.bfloat16).astype(jnp.float32)
    return high, middle, rest - middle


def scan_row(row, combine, neutral):
    lane = lax.broadcasted_iota(jnp.int32, (8, 128), 1)
    sub = lax.broadcasted_iota(jnp.int32, (8, 128), 0)
    chunk = jnp.concatenate([row[:, at * 128 : at * 128 + 128] for at in range(QUAD // 128)], axis=0)
    for step in (1, 2, 4, 8, 16, 32, 64):
        chunk = combine(chunk, jnp.where(lane >= step, pltpu.roll(chunk, step, 1), neutral))
    before = jnp.broadcast_to(chunk[:, 127:], (8, 128))
    before = jnp.where(sub >= 1, pltpu.roll(before, 1, 0), neutral)
    for step in (1, 2, 4):
        before = combine(before, jnp.where(sub >= step, pltpu.roll(before, step, 0), neutral))
    chunk = combine(chunk, before)
    return jnp.concatenate([chunk[at : at + 1, :] for at in range(QUAD // 128)], axis=1)


def assemble(core, own_ref, other_ref, weight_ref):
    for part in range(4):
        for z in range(NZ):
            columns = pl.ds(part * 128, 128)
            weight_ref[z, core, :, columns] = own_ref[part, z, :HALF, :]
            weight_ref[z, 1 - core, :, columns] = other_ref[part, z, :HALF, :]
    mine = jnp.sum(own_ref[0, :, HALF:, :].astype(jnp.float32), axis=1)
    theirs = jnp.sum(other_ref[0, :, HALF:, :].astype(jnp.float32), axis=1)
    first = jnp.where(core == 0, mine, theirs)
    second = jnp.where(core == 0, theirs, mine)
    inputs = jnp.concatenate([first[:, :HALF], second[:, :HALF]], axis=1)
    forgets = jnp.concatenate([first[:, HALF:], second[:, HALF:]], axis=1)
    row = lax.broadcasted_iota(jnp.int32, (128, 128), 0)
    for z in range(NZ):
        rows = jnp.where(row == 0, inputs[z : z + 1], jnp.where(row == 1, forgets[z : z + 1], 0.0))
        columns = rows.T.astype(jnp.bfloat16).reshape(NC, HALF, 128)
        weight_ref[z, :, :, 2 * DK + DV :] = columns


def project_kernel(
    info,
    bias,
    x_ref,
    near_ref,
    far_ref,
    head_ref,
    tail_ref,
    own_ref,
    other_ref,
    q_ref,
    kt_ref,
    v_ref,
    rows_ref,
    sent_ref,
    weight_ref,
    pre_ref,
    scaling_ref,
):
    assemble(info[0], own_ref, other_ref, weight_ref)
    across = jnp.concatenate([head_ref[...], tail_ref[...]], axis=0)
    tokens = {0: x_ref[0], 1: near_ref[...], 3: far_ref[...], 2: across}
    places = {
        swap: pl.ds(pl.multiple_of(jnp.bitwise_xor(info[3], swap) * TOK, TOK), TOK)
        for swap in tokens
    }
    for swap, part in tokens.items():
        gates = dot(part, weight_ref[:, :, :, 2 * DK + DV :].reshape(D, 128))
        pre_ref[:, places[swap]] = gates.T[:8, :]

    live = info[2] * QUAD + lax.broadcasted_iota(jnp.int32, (1, QUAD), 1) < info[1]
    forget_pre = pre_ref[1:2, :] + bias[0]
    log_sigmoid = jnp.minimum(forget_pre, 0.0) - jnp.log1p(jnp.exp(-jnp.abs(forget_pre)))
    log_forget = jnp.where(live, log_sigmoid, 0.0)
    log_input = jnp.where(live, pre_ref[0:1, :], lowest)
    decay_sum = scan_row(log_forget, jnp.add, 0.0)
    relative = log_input - decay_sum
    running_top = scan_row(relative, jnp.maximum, 2 * lowest)
    total = decay_sum[:, QUAD - 1 :]
    last_top = running_top[:, QUAD - 1 :]
    rows_ref[...] = jnp.concatenate(
        [relative, running_top, jnp.zeros((6, QUAD), jnp.float32)], axis=0
    )
    scaling_ref[0:1, :] = jnp.where(live, jnp.exp(relative - last_top), 0.0)

    memory = jnp.zeros((DK, DV), jnp.float32)
    normal = jnp.zeros((DK, TOK), jnp.float32)
    for swap, part in tokens.items():
        here = places[swap]
        projected = dot(part, weight_ref[:, :, :, : 2 * DK + DV].reshape(D, 2 * DK + DV))
        keys = projected[:, DK : 2 * DK].astype(jnp.bfloat16).T
        values = projected[:, 2 * DK :].astype(jnp.bfloat16)
        q_ref[here, :] = projected[:, :DK].astype(jnp.bfloat16)
        kt_ref[:, here] = keys
        v_ref[here, :] = values
        weighted = keys.astype(jnp.float32) * scaling_ref[0:1, here]
        normal = normal + weighted
        memory = memory + dot(weighted.astype(jnp.bfloat16), values)
    normal = jnp.sum(normal, axis=1, keepdims=True)
    lane = lax.broadcasted_iota(jnp.int32, (DK, 128), 1)
    logs = jnp.where(lane == 0, normal, 0.0)
    for at, value in enumerate((*split3(total), *split3(total + last_top))):
        logs = jnp.where(lane == at + 1, value, logs)
    for to in range(NX):
        sent_ref[to, :, :DV] = memory.astype(jnp.bfloat16)
        sent_ref[to, :, DV:] = logs.astype(jnp.bfloat16)


def cell_kernel(info, q_ref, kt_ref, v_ref, rows_ref, states_ref, out_ref):
    place = info[2]
    state = jnp.zeros((DK, EXT), jnp.float32)
    carry_top = jnp.full((1, 1), lowest, jnp.float32)
    for source in range(NX - 1):
        entry = states_ref[source].astype(jnp.float32)
        logs = entry[0:1, DV:]
        total = logs[:, 1:2] + (logs[:, 2:3] + logs[:, 3:4])
        top_part = logs[:, 4:5] + (logs[:, 5:6] + logs[:, 6:7])
        top_new = jnp.maximum(total + carry_top, top_part)
        joined = jnp.exp(total + carry_top - top_new) * state + jnp.exp(top_part - top_new) * entry
        state = jnp.where(source < place, joined, state)
        carry_top = jnp.where(source < place, top_new, carry_top)
    carried = state.astype(jnp.bfloat16)

    scale = DK**-0.5
    columns = rows_ref[...].T
    for block in range(NY):
        here = pl.ds(block * TOK, TOK)
        extent = (block + 1) * TOK
        top = jnp.maximum(columns[block * TOK : extent, 1:2], carry_top)
        queries = q_ref[here, :]
        scores = dot(queries, kt_ref[:, :extent]) * scale
        relative = rows_ref[0:1, :extent] - top
        row = block * TOK + lax.broadcasted_iota(jnp.int32, (TOK, extent), 0)
        column = lax.broadcasted_iota(jnp.int32, (TOK, extent), 1)
        products = jnp.exp(jnp.where(row >= column, relative, lowest)) * scores
        carry = dot(queries, carried) * (jnp.exp(carry_top - top) * scale)
        denominator = jnp.sum(products, axis=1, keepdims=True) + carry[:, DV : DV + 1]
        numerator = dot(products.astype(jnp.bfloat16), v_ref[:extent, :]) + carry[:, :DV]
        result = numerator / jnp.maximum(jnp.abs(denominator), 1.0)
        at = place * QUAD + block * TOK + lax.broadcasted_iota(jnp.int32, (TOK, 1), 0)
        out_ref[block] = jnp.where(at < info[1], result, 0.0).astype(jnp.bfloat16)


def merge_kernel(heads_ref, out_ref):
    for head in range(H):
        out_ref[0, :, head * DV : (head + 1) * DV] = heads_ref[head]


SMEM = pl.BlockSpec(memory_space=pltpu.SMEM)
VMEM = pl.BlockSpec(memory_space=pltpu.VMEM)


def granted(mebibytes):
    return pltpu.CompilerParams(vmem_limit_bytes=mebibytes * 1024 * 1024)


def shaped(*shape, dtype=jnp.bfloat16):
    return jax.ShapeDtypeStruct(shape, dtype)


def project(info, bias, tokens, own, other, **options):
    return pl.pallas_call(
        project_kernel,
        out_shape=(
            shaped(QUAD, DK),
            shaped(DK, QUAD),
            shaped(QUAD, DV),
            shaped(8, QUAD, dtype=jnp.float32),
            shaped(NX, DK, EXT),
        ),
        in_specs=[SMEM, SMEM] + [VMEM] * 7,
        out_specs=(VMEM,) * 5,
        scratch_shapes=[
            pltpu.VMEM((NZ, NC, HALF, WIDE), jnp.bfloat16),
            pltpu.VMEM((8, QUAD), jnp.float32),
            pltpu.VMEM((8, QUAD), jnp.float32),
        ],
        compiler_params=granted(49),
        name="project",
        **options,
    )(info, bias, *tokens, own, other)


def cell(info, q, kt, v, rows, states, **options):
    return pl.pallas_call(
        cell_kernel,
        out_shape=shaped(NY, TOK, DV),
        in_specs=[SMEM] + [VMEM] * 5,
        out_specs=VMEM,
        compiler_params=granted(16),
        name="cell",
        **options,
    )(info, q, kt, v, rows, states)


def merge(heads, **options):
    return pl.pallas_call(
        merge_kernel,
        out_shape=shaped(1, TOK, H * DV),
        in_specs=[VMEM],
        out_specs=VMEM,
        compiler_params=granted(8),
        name="merge",
        **options,
    )(heads)


def piece_kernel(place, proj_ref, gate_ref, out_ref):
    x, y = place[0], place[1]
    for quarter, at in enumerate((y, H + y, 2 * H + 2 * y, 2 * H + 2 * y + 1)):

        @pl.when(x == quarter)
        def _(at=at):
            out_ref[0, :HALF, :] = proj_ref[:, pl.ds(pl.multiple_of(at * 128, 128), 128)]

    gates = gate_ref[...].astype(jnp.float32)
    column = lax.broadcasted_iota(jnp.int32, (2 * H, HALF), 0)
    inputs = jnp.sum(jnp.where(column == y, gates, 0.0), axis=0, keepdims=True)
    forgets = jnp.sum(jnp.where(column == H + y, gates, 0.0), axis=0, keepdims=True)
    both = jnp.concatenate([inputs, forgets], axis=1)
    row = lax.broadcasted_iota(jnp.int32, (8, 128), 0)
    out_ref[0, HALF:, :] = jnp.where(row == 0, both, 0.0).astype(jnp.bfloat16)
    for to in range(1, NZ):
        out_ref[to] = out_ref[0]


def weight_piece(place, proj_weight, gate_weight, **options):
    return pl.pallas_call(
        piece_kernel,
        out_shape=shaped(NZ, PIECE, 128),
        in_specs=[SMEM, VMEM, VMEM],
        out_specs=VMEM,
        compiler_params=granted(8),
        name="piece",
        **options,
    )(place, proj_weight, gate_weight.T)


def swap_along(array, axis, swap):
    return lax.ppermute(array, axis, [(i, i ^ swap) for i in range(4)])


def per_device(activations, proj_weight, gate_weight, forget_bias, accepted):
    x, y, core = (lax.axis_index(a) for a in ("x", "y", "c"))
    own_tokens = activations[0]
    near = swap_along(own_tokens, "y", 1)
    far = swap_along(own_tokens, "y", 3)
    head = swap_along(near[:CUT], "y", 3)
    tail = swap_along(far[CUT:], "y", 1)
    place = jnp.stack([x, y]).astype(jnp.int32)
    rows = lax.all_to_all(weight_piece(place, proj_weight, gate_weight), "z", 0, 0)
    own = lax.all_to_all(jnp.tile(rows.reshape(1, NZ * PIECE, 128), (NX, 1, 1)), "x", 0, 0)
    own, head, tail = lax.optimization_barrier((own.reshape(NX * NZ * PIECE, 128), head, tail))
    other = lax.ppermute(own, "c", [(0, 1), (1, 0)])
    shape = (4, NZ, PIECE, 128)
    info = jnp.stack([core, accepted[0], x, y]).astype(jnp.int32)
    bias = lax.dynamic_slice(forget_bias, (y,), (1,))
    tokens = (activations, near, far, head, tail)
    q, kt, v, gates, sent = project(info, bias, tokens, own.reshape(shape), other.reshape(shape))
    states = lax.all_to_all(sent, "x", 0, 0, tiled=True)
    out = cell(info, q, kt, v, gates, states)
    return merge(lax.all_to_all(out, "y", 0, 0, tiled=True))


def solution(mesh):
    axes = Mesh(mesh.devices.reshape(NX, NY, NZ, NC), ("x", "y", "z", "c"))
    tokens = P(("z", "c"), ("x", "y"), None)
    weights = P(("z", "c"), None)
    return jax.shard_map(
        per_device,
        mesh=axes,
        in_specs=(tokens, weights, weights, P(), P(("z", "c"))),
        out_specs=tokens,
        check_vma=False,
    )
```
